256 devices in a mesh: dp: 32 (over z, x), tensor: 8 (over y, core).
Axes of the slice: x: 4, y: 4, z: 8, core: 2. Of those that a mesh axis runs over, the one named last changes fastest.
Arguments:
- grads: bfloat16 [32, 2, 4096, 1024], P('dp', None, None, 'tensor'), may hold values from -6 to 6
- momentum: bfloat16 [32, 2, 4096, 1024], P('dp', None, None, 'tensor'), may hold values from -6 to 6
- error: bfloat16 [32, 2, 4096, 1024], P('dp', None, None, 'tensor'), may hold values from -4 to 4
- q_warm: bfloat16 [1024, 128], P('tensor'), may hold values from -0.1875 to 0.1875
Outputs:
- momentum_out: bfloat16 [32, 2, 4096, 1024], P('dp', None, None, 'tensor')
- error_out: bfloat16 [32, 2, 4096, 1024], P('dp', None, None, 'tensor')
- p_factor: bfloat16 [4096, 128], replicated
- q_factor: float32 [1024, 128], P('tensor')
The draws below stay inside these ranges and needn't reach their ends.
All inputs are finite; a program needn't handle non-finite values.
Results may differ from the reference program's by a relative error of at most 0.017.
Values may be sent and summed in bfloat16 or wider, within the bound.
No kernel may reach another device: no remote copies, remote signals or barrier semaphores. Data moves between devices by JAX's collectives and lax.ppermute only.
A program may use at most 64 MiB of HBM per device.

```python
import jax
import jax.numpy as jnp
from jax import lax

ROWS = 4096
RANK = 64
KVW = 1024
REPLICAS = 32
N_DP = 32


def level_of(own_key, extent, cuts, low, high):
    level, own = 1.0, jax.random.fold_in(own_key, 6)
    for position, blocks in cuts:
        heights = jnp.exp(jax.random.uniform(jax.random.fold_in(own, position), (blocks,), jnp.float32, low / len(cuts), high / len(cuts)))
        level = level * jnp.repeat(heights, extent[position] // blocks).reshape([-1 if axis == position else 1 for axis in range(len(extent))])
    return level


def normal_values(own_key, dims, deviation, most, cuts=(), dtype=jnp.bfloat16):
    factor_of = level_of(own_key, dims, cuts, -0.22, 0.18) if cuts else 1.0
    result = jax.random.normal(own_key, dims, jnp.float32) * deviation * factor_of
    return jnp.minimum(jnp.maximum(result, -most), most).astype(dtype)


def setup_inputs(seed: int = 0) -> dict:
    streams_of = jax.random.split(jax.random.key(seed), 5)
    return {
        "grads": normal_values(streams_of[0], (REPLICAS, 2, ROWS, KVW), 1.0, 6.0, ((0, 32), (3, 8))),
        "momentum": normal_values(streams_of[1], (REPLICAS, 2, ROWS, KVW), 1.0, 6.0, ((0, 32), (3, 8))),
        "error": normal_values(streams_of[2], (REPLICAS, 2, ROWS, KVW), 0.5, 4.0, ((0, 32), (3, 8))),
        "q_warm": normal_values(streams_of[3], (KVW, 2 * RANK), KVW ** -0.5, 0.1875, ((0, 8),)),
    }


def reference(grads, momentum, error, q_warm):
    momentum_out = (0.9 * momentum.astype(jnp.float32) + grads.astype(jnp.float32)).astype(jnp.bfloat16)
    corrected = (momentum_out.astype(jnp.float32) + error.astype(jnp.float32)).astype(jnp.bfloat16)
    q_three = q_warm.astype(jnp.float32).reshape(KVW, 2, RANK)

    def p_term(carry, block):
        return (carry + jnp.einsum('grk,kgn->rgn', block.astype(jnp.float32), q_three), None)
    p_raw, _ = lax.scan(p_term, jnp.zeros((ROWS, 2, RANK), jnp.float32), corrected)
    gram = jnp.einsum('rgn,rgm->gnm', p_raw, p_raw, precision=lax.Precision.HIGHEST)
    pieces = []
    for group in range(2):
        lower = jnp.linalg.cholesky(gram[group])
        pieces.append(lax.linalg.triangular_solve(lower, p_raw[:, group, :], left_side=False, lower=True, transpose_a=True))
    p_factor = jnp.stack(pieces, 1).reshape(ROWS, 2 * RANK).astype(jnp.bfloat16)
    p_three = p_factor.astype(jnp.float32).reshape(ROWS, 2, RANK)

    def q_term(carry, block):
        return (carry + jnp.einsum('grk,rgn->kgn', block.astype(jnp.float32), p_three), None)
    q_total, _ = lax.scan(q_term, jnp.zeros((KVW, 2, RANK), jnp.float32), corrected)
    q_factor = (q_total / N_DP).reshape(KVW, 2 * RANK)
    q_round = lax.optimization_barrier(q_factor.astype(jnp.bfloat16)).astype(jnp.float32)
    approx = jnp.einsum('rgn,kgn->grk', p_three, q_round.reshape(KVW, 2, RANK))
    error_out = (corrected.astype(jnp.float32) - approx[None]).astype(jnp.bfloat16)
    return (momentum_out, error_out, p_factor, q_factor)
```

```python
import jax
import jax.numpy as jnp
from jax import lax
from jax.experimental import pallas as pl
from jax.experimental.pallas import tpu as pltpu
from jax.sharding import Mesh
from jax.sharding import PartitionSpec as P

BF, F32 = jnp.bfloat16, jnp.float32
NZ, NX, NY, NC = 8, 4, 4, 2
ROWS, COLS, RANK2 = 4096, 128, 128
HALF = ROWS // NC
BLK = HALF // (NX * NY)
STEP = 512
NSTEP = HALF // STEP
MIB = 1 << 20


def dot(a, b, dims=((1,), (0,)), precision=None):
    return lax.dot_general(a, b, (dims, ((), ())), precision=precision, preferred_element_type=F32)


def left_lanes(shape):
    return lax.broadcasted_iota(jnp.int32, shape, len(shape) - 1) < RANK2 // 2


def front_body(half_ref, g_ref, m_ref, e_ref, q_ref, *rest):
    mo_ref, co_ref, p_ref = rest[-3:]
    q = q_ref[...]
    left = left_lanes(q.shape)
    total = None
    for group in range(2):
        mo = (0.9 * m_ref[0, group].astype(F32) + g_ref[0, group].astype(F32)).astype(BF)
        co = (mo.astype(F32) + e_ref[0, group].astype(F32)).astype(BF)
        mo_ref[0, group] = mo
        co_ref[group] = co
        term = dot(co, jnp.where(left if group == 0 else ~left, q, jnp.zeros_like(q)))
        total = term if total is None else total + term
    p_ref[...] = total.astype(p_ref.dtype)


def front(half, grads, momentum, error, q_warm, before, p_dtype):
    big = pl.BlockSpec((1, 2, STEP, COLS), lambda i, h: (0, 0, h[0] * NSTEP + i, 0))
    in_specs = [big, big, big, pl.BlockSpec((COLS, RANK2), lambda i, h: (0, 0))]
    args = [grads, momentum, error, q_warm]
    aliases = {}
    if before is not None:
        in_specs.append(pl.BlockSpec(memory_space=pl.ANY))
        args.append(before)
        aliases = {5: 0}
    return pl.pallas_call(
        front_body,
        grid_spec=pltpu.PrefetchScalarGridSpec(
            num_scalar_prefetch=1,
            grid=(NSTEP,),
            in_specs=in_specs,
            out_specs=[
                big,
                pl.BlockSpec((2, STEP, COLS), lambda i, h: (0, i, 0)),
                pl.BlockSpec((STEP, RANK2), lambda i, h: (i, 0)),
            ],
        ),
        out_shape=[
            jax.ShapeDtypeStruct(grads.shape, BF),
            jax.ShapeDtypeStruct((2, HALF, COLS), BF),
            jax.ShapeDtypeStruct((HALF, RANK2), p_dtype),
        ],
        input_output_aliases=aliases,
        compiler_params=pltpu.CompilerParams(vmem_limit_bytes=16 * MIB),
        cost_estimate=pl.CostEstimate(flops=2 * HALF * 256 * 128, bytes_accessed=6 * MIB, transcendentals=0),
    )(half, *args)


def sum_copies_body(x_ref, o_ref):
    total = x_ref[0].astype(F32)
    for k in range(1, x_ref.shape[0]):
        total = total + x_ref[k].astype(F32)
    total = total.astype(BF)
    for k in range(o_ref.shape[0]):
        o_ref[k] = total


def sum_copies(x, copies):
    return pl.pallas_call(
        sum_copies_body,
        out_shape=jax.ShapeDtypeStruct((copies, *x.shape[1:]), BF),
        compiler_params=pltpu.CompilerParams(vmem_limit_bytes=16 * MIB),
    )(x)


def products_body(p_ref, c_ref, *rest):
    u_ref, g_ref = rest[-2:]
    u0 = u1 = gram = None
    for i in range(NSTEP):
        rows = pl.ds(i * STEP, STEP)
        p = p_ref[rows]
        pt = p.T
        a, b, c = dot(pt[: RANK2 // 2], c_ref[0, rows]), dot(pt[RANK2 // 2 :], c_ref[1, rows]), dot(pt, p)
        u0, u1, gram = (a, b, c) if u0 is None else (u0 + a, u1 + b, gram + c)
    u = jnp.concatenate([u0, u1], axis=0)
    if len(rest) == 2:
        u_ref[...] = u
        g_ref[...] = gram
    else:
        u = (u + rest[0][...]).astype(BF)
        for k in range(NZ):
            u_ref[k] = u
        g_ref[...] = gram + rest[1][...]


def products(p, c, before):
    last = before is not None
    return pl.pallas_call(
        products_body,
        out_shape=[
            jax.ShapeDtypeStruct((NZ, RANK2, COLS) if last else (RANK2, COLS), BF if last else F32),
            jax.ShapeDtypeStruct((RANK2, RANK2), F32),
        ],
        compiler_params=pltpu.CompilerParams(vmem_limit_bytes=16 * MIB),
        cost_estimate=pl.CostEstimate(flops=2 * HALF * 256 * 128, bytes_accessed=2 * MIB, transcendentals=0),
    )(p, c, *(before if last else ()))


def inverse_body(g_ref, o_ref):
    n = RANK2 // 2
    gram = g_ref[...]
    row = lax.broadcasted_iota(jnp.int32, (n, 2 * n), 0)
    lane = lax.broadcasted_iota(jnp.int32, (n, 2 * n), 1)
    eye_left = jnp.where(row == lane, 1.0, 0.0)
    eye_right = jnp.where(row + n == lane, 1.0, 0.0)
    left = lane < n
    top = jnp.where(left, gram[:n], eye_right)
    swapped = pltpu.roll(gram[n:], n, 1)
    bottom = jnp.where(left, swapped, eye_right)
    both = [top, bottom]
    for k in range(n - 1):
        for s in range(2):
            a = both[s]
            pivot = a[k : k + 1, :]
            column = a[:, k : k + 1]
            factor = jnp.where(row[:, :1] > k, column / a[k : k + 1, k : k + 1], 0.0)
            both[s] = a - factor * pivot
    out = []
    for s in range(2):
        a = both[s]
        d = jnp.sum(a * eye_left, axis=1, keepdims=True)
        out.append(a * lax.rsqrt(d))
    o_ref[:n] = jnp.where(left, pltpu.roll(out[0], n, 1), 0.0)
    o_ref[n:] = jnp.where(left, 0.0, out[1])


def inverse(gram):
    return pl.pallas_call(
        inverse_body,
        out_shape=jax.ShapeDtypeStruct((RANK2, RANK2), F32),
        compiler_params=pltpu.CompilerParams(vmem_limit_bytes=16 * MIB),
        cost_estimate=pl.CostEstimate(flops=4 * 64**3, bytes_accessed=128 * 1024, transcendentals=128),
    )(gram)


def back_body(half_ref, po_ref, pt_ref, co_ref, ct_ref, l_ref, u_ref, e_ref, p_ref, q_ref, qt_ref, hi_ref, lo_ref):
    i = pl.program_id(0)

    @pl.when(i == 0)
    def _():
        inv = l_ref[...]
        qt = dot(inv, u_ref[...], precision=lax.Precision.HIGHEST) * (1.0 / (NZ * NX))
        q_ref[...] = qt.T
        qt_ref[...] = qt.astype(BF)
        hi = inv.astype(BF)
        hi_ref[...] = hi
        lo_ref[...] = (inv - hi.astype(F32)).astype(BF)

    def part(p_in, c_in):
        p = p_in[...]
        factor = dot(p, hi_ref[...], ((1,), (1,))) + dot(p, lo_ref[...], ((1,), (1,)))
        factor = factor.astype(BF)
        p_ref[...] = factor
        n = RANK2 // 2
        for group in range(2):
            approx = dot(factor[:, group * n : (group + 1) * n], qt_ref[group * n : (group + 1) * n])
            e_ref[0, group] = (c_in[group].astype(F32) - approx).astype(BF)

    @pl.when(i < NSTEP)
    def _():
        part(po_ref, co_ref)

    @pl.when(i >= NSTEP)
    def _():
        part(pt_ref, ct_ref)


def back(half, p_own, p_other, c_own, c_other, inv, u):
    def own(i):
        return jnp.minimum(i, NSTEP - 1)

    def other(i):
        return jnp.maximum(i - NSTEP, 0)

    def where(i, h):
        return jnp.where(i < NSTEP, h[0] * NSTEP + i, (1 - h[0]) * NSTEP + i - NSTEP)

    small = pl.BlockSpec((RANK2, RANK2), lambda i, h: (0, 0))
    return pl.pallas_call(
        back_body,
        grid_spec=pltpu.PrefetchScalarGridSpec(
            num_scalar_prefetch=1,
            grid=(2 * NSTEP,),
            in_specs=[
                pl.BlockSpec((STEP, RANK2), lambda i, h: (own(i), 0)),
                pl.BlockSpec((STEP, RANK2), lambda i, h: (other(i), 0)),
                pl.BlockSpec((2, STEP, COLS), lambda i, h: (0, own(i), 0)),
                pl.BlockSpec((2, STEP, COLS), lambda i, h: (0, other(i), 0)),
                small,
                small,
            ],
            out_specs=[
                pl.BlockSpec((1, 2, STEP, COLS), lambda i, h: (0, 0, where(i, h), 0)),
                pl.BlockSpec((STEP, RANK2), lambda i, h: (where(i, h), 0)),
                small,
            ],
            scratch_shapes=[pltpu.VMEM((RANK2, COLS), BF), pltpu.VMEM((RANK2, RANK2), BF), pltpu.VMEM((RANK2, RANK2), BF)],
        ),
        out_shape=[
            jax.ShapeDtypeStruct((1, 2, ROWS, COLS), BF),
            jax.ShapeDtypeStruct((ROWS, RANK2), BF),
            jax.ShapeDtypeStruct((COLS, RANK2), F32),
        ],
        compiler_params=pltpu.CompilerParams(vmem_limit_bytes=16 * MIB),
        cost_estimate=pl.CostEstimate(flops=6 * ROWS * 128 * 128, bytes_accessed=8 * MIB, transcendentals=0),
    )(half, p_own, p_other, c_own, c_other, inv, u)


def swap_cores(x):
    return lax.ppermute(x, "c", [(0, 1), (1, 0)])


def exchange(x, axes):
    return lax.all_to_all(x, axes, 0, 0)


def local(grads, momentum, error, q_warm):
    c = lax.axis_index("c").astype(jnp.int32)
    mine, theirs = c.reshape(1), (1 - c).reshape(1)

    with jax.named_scope("p_partial"):
        mo, c_other, p_send = front(theirs, grads, momentum, error, q_warm, None, BF)
        p_got = swap_cores(p_send)
        momentum_out, c_own, p_own = front(mine, grads, momentum, error, q_warm, mo, F32)
        chip = (p_own + p_got.astype(F32)).astype(BF)
    with jax.named_scope("p_sum"):
        parts = exchange(chip.reshape(NX * NY, BLK, RANK2), ("x", "y"))
        parts = exchange(sum_copies(parts, NZ), "z")
        p_mine = exchange(sum_copies(parts, NX * NY), ("x", "y")).reshape(HALF, RANK2)
        p_theirs = swap_cores(p_mine)
    with jax.named_scope("u_sum"):
        first = products(p_mine, c_own, None)
        copies, gram = products(p_theirs, c_other, first)
        parts = exchange(copies, "z")
        u = jnp.sum(parts.astype(F32), axis=0).astype(BF)
        got = [lax.ppermute(u, "x", [(i, i ^ k) for i in range(NX)]) for k in (1, 2, 3)]
        inv = inverse(gram)
        u, a, b, d = (t.astype(F32) for t in (u, *got))
        u = (u + a) + (b + d)
    with jax.named_scope("back"):
        error_out, p_factor, q_factor = back(mine, p_mine, p_theirs, c_own, c_other, inv, u)
    return momentum_out, error_out, p_factor, q_factor


def solution(mesh):
    fine = Mesh(mesh.devices.reshape(NZ, NX, NY, NC), ("z", "x", "y", "c"))
    dp, tensor = ("z", "x"), ("y", "c")
    big = P(dp, None, None, tensor)
    return jax.shard_map(
        local,
        mesh=fine,
        in_specs=(big, big, big, P(tensor, None)),
        out_specs=(big, big, P(), P(tensor, None)),
        check_vma=False,
    )
```

```python
import jax
import jax.numpy as jnp
from jax import lax
from jax.experimental import pallas as pl
from jax.experimental.pallas import tpu as pltpu
from jax.sharding import Mesh
from jax.sharding import PartitionSpec as P

BF, F32 = jnp.bfloat16, jnp.float32
NZ, NX, NY, NC = 8, 4, 4, 2
ROWS, COLS, RANK2 = 4096, 128, 128
HALF = ROWS // NC
BLK = HALF // (NX * NY)
FRONT, PROD, BACK = 1024, 512, 512
PANEL = 8
MIB = 1 << 20


def dot(a, b, dims=((1,), (0,)), precision=None):
    return lax.dot_general(a, b, (dims, ((), ())), precision=precision, preferred_element_type=F32)


def left_lanes(shape):
    return lax.broadcasted_iota(jnp.int32, shape, len(shape) - 1) < RANK2 // 2


def front_body(half_ref, g_hbm, m_hbm, e_hbm, q_hbm, mo_ref, c_ref, p_ref, g_buf, m_buf, e_buf, q_buf, sem, q_sem):
    base = pl.multiple_of(half_ref[0] * HALF, HALF)

    def loads(k):
        here = pl.ds(pl.multiple_of(k * FRONT, FRONT), FRONT)
        there = pl.ds(pl.multiple_of(base + k * FRONT, FRONT), FRONT)
        return [
            pltpu.make_async_copy(hbm.at[0, :, there], buf.at[:, here], sem.at[i, k])
            for i, (hbm, buf) in enumerate(((m_hbm, m_buf), (g_hbm, g_buf), (e_hbm, e_buf)))
        ]

    load_q = pltpu.make_async_copy(q_hbm, q_buf, q_sem)
    load_q.start()
    for k in range(HALF // FRONT):
        for copy in loads(k):
            copy.start()
    load_q.wait()
    q = q_buf[...]
    left = left_lanes(q.shape)
    q_of = [jnp.where(left if group == 0 else ~left, q, jnp.zeros_like(q)) for group in range(2)]

    for k in range(HALF // FRONT):
        for copy in loads(k):
            copy.wait()
        rows = pl.ds(pl.multiple_of(k * FRONT, FRONT), FRONT)
        total = None
        for group in range(2):
            mo = (0.9 * m_buf[group, rows].astype(F32) + g_buf[group, rows].astype(F32)).astype(BF)
            co = (mo.astype(F32) + e_buf[group, rows].astype(F32)).astype(BF)
            mo_ref[group, rows] = mo
            c_ref[group, rows] = co
            term = dot(co, q_of[group])
            total = term if total is None else total + term
        p_ref[rows] = total.astype(p_ref.dtype)


def front(half, args, p_dtype):
    hbm, vmem = pl.BlockSpec(memory_space=pltpu.HBM), pl.BlockSpec(memory_space=pltpu.VMEM)
    return pl.pallas_call(
        front_body,
        in_specs=[pl.BlockSpec(memory_space=pltpu.SMEM)] + [hbm] * 4,
        out_specs=[vmem] * 3,
        out_shape=[pltpu.VMEM((2, HALF, COLS), BF), pltpu.VMEM((2, HALF, COLS), BF), pltpu.VMEM((HALF, RANK2), p_dtype)],
        scratch_shapes=[pltpu.VMEM((2, HALF, COLS), BF)] * 3
        + [pltpu.VMEM((COLS, RANK2), BF), pltpu.SemaphoreType.DMA((3, HALF // FRONT)), pltpu.SemaphoreType.DMA],
        compiler_params=pltpu.CompilerParams(vmem_limit_bytes=16 * MIB),
        cost_estimate=pl.CostEstimate(flops=2 * HALF * 256 * 128, bytes_accessed=4 * MIB, transcendentals=0),
    )(half, *(pltpu.with_memory_space_constraint(x, pltpu.HBM) for x in args))


def sum_copies_body(x_ref, o_ref):
    total = x_ref[0].astype(F32)
    for k in range(1, x_ref.shape[0]):
        total = total + x_ref[k].astype(F32)
    total = total.astype(BF)
    for k in range(o_ref.shape[0]):
        o_ref[k] = total


def sum_copies(x, copies):
    return pl.pallas_call(
        sum_copies_body,
        out_shape=jax.ShapeDtypeStruct((copies, *x.shape[1:]), BF),
        compiler_params=pltpu.CompilerParams(vmem_limit_bytes=16 * MIB),
    )(x)


def products_body(p_ref, c_ref, *rest):
    u_ref, g_ref = rest[-2:]
    n = RANK2 // 2
    u0 = u1 = gram = None
    for k in range(HALF // PROD):
        rows = pl.ds(k * PROD, PROD)
        p = p_ref[rows]
        pt = p.T
        a, b, c = dot(pt[:n], c_ref[0, rows]), dot(pt[n:], c_ref[1, rows]), dot(pt, p)
        u0, u1, gram = (a, b, c) if u0 is None else (u0 + a, u1 + b, gram + c)
    u = jnp.concatenate([u0, u1], axis=0)
    if len(rest) == 2:
        u_ref[...] = u
        g_ref[...] = gram
    else:
        u = (u + rest[0][...]).astype(BF)
        for k in range(NZ):
            u_ref[k] = u
        g_ref[...] = gram + rest[1][...]


def products(p, c, before):
    last = before is not None
    return pl.pallas_call(
        products_body,
        out_shape=[
            jax.ShapeDtypeStruct((NZ, RANK2, COLS) if last else (RANK2, COLS), BF if last else F32),
            jax.ShapeDtypeStruct((RANK2, RANK2), F32),
        ],
        compiler_params=pltpu.CompilerParams(vmem_limit_bytes=16 * MIB),
        cost_estimate=pl.CostEstimate(flops=2 * HALF * 256 * 128, bytes_accessed=2 * MIB, transcendentals=0),
    )(p, c, *(before if last else ()))


def inverse_rows(g_ref):
    n, t = RANK2 // 2, PANEL
    tiles = n // t
    lane = lax.broadcasted_iota(jnp.int32, (t, 2 * n), 1)
    sub = lax.broadcasted_iota(jnp.int32, (t, 2 * n), 0)
    left = lane < n

    def spread(x):
        return jnp.broadcast_to(x, (t, 2 * n))

    both, pivots = [], [[None] * tiles for _ in range(2)]
    for s in range(2):
        own = []
        for i in range(tiles):
            x = g_ref[s * n + t * i : s * n + t * i + t]
            x = pltpu.roll(x, n, 1) if s else x
            own.append(jnp.where(left, x, jnp.where(lane == sub + (t * i + n), 1.0, 0.0)))
        both.append(own)
    for top in range(tiles):
        columns = [
            [[spread(a[i][:, top * t + j : top * t + j + 1]) if i >= top else None for i in range(tiles)] for j in range(t)]
            for a in both
        ]
        for j in range(t):
            for s in range(2):
                c, a = columns[s], both[s]
                d = spread(c[j][top][j : j + 1])
                pivots[s][top] = d if j == 0 else jnp.where(sub == j, d, pivots[s][top])
                scale = 1.0 / d
                row = spread(a[top][j : j + 1])
                later = [spread(c[j][top][q : q + 1]) for q in range(j + 1, t)]
                for i in range(top, tiles):
                    factor = c[j][i] * scale
                    if i == top:
                        factor = jnp.where(sub > j, factor, 0.0)
                    for q, value in enumerate(later, j + 1):
                        c[q][i] = c[q][i] - factor * value
                    a[i] = a[i] - factor * row
    out = []
    for s in range(2):
        for i in range(tiles):
            y = both[s][i] * lax.rsqrt(pivots[s][i])
            out.append(jnp.where(left, 0.0, y) if s else jnp.where(left, pltpu.roll(y, n, 1), 0.0))
    return out


def factor_body(half_ref, g_ref, po_ref, pt_ref, mo_ref, mt_ref, m_hbm, p_hbm, f_ref, l_ref, w_ref, sem, m_sem):
    halves = [pl.multiple_of(h * HALF, HALF) for h in (half_ref[0], 1 - half_ref[0])]
    moves = [
        pltpu.make_async_copy(ref, m_hbm.at[0, :, pl.ds(halves[i], HALF)], m_sem.at[i]) for i, ref in enumerate((mo_ref, mt_ref))
    ]
    for copy in moves:
        copy.start()
    for i, rows in enumerate(inverse_rows(g_ref)):
        l_ref[i * PANEL : (i + 1) * PANEL] = rows
    inv_t = l_ref[...].T
    hi = inv_t.astype(BF)
    w_ref[:RANK2] = hi
    w_ref[RANK2:] = (inv_t - hi.astype(F32)).astype(BF)
    weights = w_ref[...]
    for which, p_ref in enumerate((po_ref, pt_ref)):
        moves.append(pltpu.make_async_copy(f_ref.at[pl.ds(which * HALF, HALF)], p_hbm.at[pl.ds(halves[which], HALF)], sem.at[which]))

        for k in range(HALF // BACK):
            p = p_ref[pl.ds(pl.multiple_of(k * BACK, BACK), BACK)]
            here = pl.ds(pl.multiple_of(which * HALF + k * BACK, BACK), BACK)
            f_ref[here] = dot(jnp.concatenate([p, p], axis=1), weights).astype(BF)

        moves[-1].start()
    for copy in moves:
        copy.wait()


def factor(half, gram, p_own, p_other, mo_own, mo_other):
    hbm, vmem = pl.BlockSpec(memory_space=pltpu.HBM), pl.BlockSpec(memory_space=pltpu.VMEM)
    return pl.pallas_call(
        factor_body,
        in_specs=[pl.BlockSpec(memory_space=pltpu.SMEM)] + [vmem] * 5,
        out_specs=[hbm, hbm, vmem, vmem],
        out_shape=[
            jax.ShapeDtypeStruct((1, 2, ROWS, COLS), BF),
            jax.ShapeDtypeStruct((ROWS, RANK2), BF),
            jax.ShapeDtypeStruct((ROWS, RANK2), BF),
            jax.ShapeDtypeStruct((RANK2, RANK2), F32),
        ],
        scratch_shapes=[pltpu.VMEM((2 * RANK2, RANK2), BF), pltpu.SemaphoreType.DMA((2,)), pltpu.SemaphoreType.DMA((2,))],
        compiler_params=pltpu.CompilerParams(vmem_limit_bytes=16 * MIB),
        cost_estimate=pl.CostEstimate(flops=4 * ROWS * 128 * 128, bytes_accessed=4 * MIB, transcendentals=128),
    )(half, gram, p_own, p_other, mo_own, mo_other)


def back_body(half_ref, f_ref, co_ref, ct_ref, l_ref, u_ref, a_ref, b_ref, d_ref, e_hbm, q_ref, e_buf, w_ref, sem):
    u, a, b, d = (t[...].astype(F32) for t in (u_ref, a_ref, b_ref, d_ref))
    qt = dot(l_ref[...], (u + a) + (b + d), precision=lax.Precision.HIGHEST) * (1.0 / (NZ * NX))
    q_ref[...] = qt.T
    qt = qt.astype(BF)
    top = lax.broadcasted_iota(jnp.int32, qt.shape, 0) < RANK2 // 2
    zero = jnp.zeros_like(qt)
    w_ref[...] = jnp.concatenate([jnp.where(top, qt, zero), jnp.where(top, zero, qt)], axis=1)
    weights = w_ref[...]

    def store(which, k):
        half = half_ref[0] if which == 0 else 1 - half_ref[0]
        here = pl.ds(pl.multiple_of(which * HALF + k * BACK, BACK), BACK)
        there = pl.ds(pl.multiple_of(half * HALF + k * BACK, BACK), BACK)
        return here, pltpu.make_async_copy(e_buf.at[:, here], e_hbm.at[0, :, there], sem.at[which, k])

    for which, c_ref in enumerate((co_ref, ct_ref)):

        for k in range(HALF // BACK):
            here, copy = store(which, k)
            approx = dot(f_ref[here], weights)
            for group in range(2):
                c = c_ref[group, pl.ds(pl.multiple_of(k * BACK, BACK), BACK)].astype(F32)
                e_buf[group, here] = (c - approx[:, group * COLS : (group + 1) * COLS]).astype(BF)
            copy.start()

    for which in range(2):

        for k in range(HALF // BACK):
            store(which, k)[1].wait()


def back(half, f, c_own, c_other, inv, us):
    vmem = pl.BlockSpec(memory_space=pltpu.VMEM)
    return pl.pallas_call(
        back_body,
        in_specs=[pl.BlockSpec(memory_space=pltpu.SMEM)] + [vmem] * 8,
        out_specs=[pl.BlockSpec(memory_space=pltpu.HBM), vmem],
        out_shape=[
            jax.ShapeDtypeStruct((1, 2, ROWS, COLS), BF),
            jax.ShapeDtypeStruct((COLS, RANK2), F32),
        ],
        scratch_shapes=[
            pltpu.VMEM((2, ROWS, COLS), BF),
            pltpu.VMEM((RANK2, 2 * COLS), BF),
            pltpu.SemaphoreType.DMA((2, HALF // BACK)),
        ],
        compiler_params=pltpu.CompilerParams(vmem_limit_bytes=16 * MIB),
        cost_estimate=pl.CostEstimate(flops=4 * ROWS * 128 * 128, bytes_accessed=6 * MIB, transcendentals=0),
    )(half, f, c_own, c_other, inv, *us)


def swap_cores(x):
    return lax.ppermute(x, "c", [(0, 1), (1, 0)])


def exchange(x, axes):
    return lax.all_to_all(x, axes, 0, 0)


def local(grads, momentum, error, q_warm):
    c = lax.axis_index("c").astype(jnp.int32)
    mine, theirs = c.reshape(1), (1 - c).reshape(1)

    with jax.named_scope("p_partial"):
        args = (grads, momentum, error, q_warm)
        mo_other, c_other, p_send = front(theirs, args, BF)
        p_got = swap_cores(p_send)
        mo_own, c_own, p_own = front(mine, args, F32)
        chip = (p_own + p_got.astype(F32)).astype(BF)
    with jax.named_scope("p_sum"):
        parts = exchange(chip.reshape(NX * NY, BLK, RANK2), ("x", "y"))
        parts = exchange(sum_copies(parts, NZ), "z")
        p_mine = exchange(sum_copies(parts, NX * NY), ("x", "y")).reshape(HALF, RANK2)
        p_theirs = swap_cores(p_mine)
    with jax.named_scope("u_sum"):
        first = products(p_mine, c_own, None)
        copies, gram = products(p_theirs, c_other, first)
        parts = exchange(copies, "z")
        u = sum_copies(parts, 1)[0]
        got = [lax.ppermute(u, "x", [(i, i ^ k) for i in range(NX)]) for k in (1, 2, 3)]
        momentum_out, p_factor, f, inv = factor(mine, gram, p_mine, p_theirs, mo_own, mo_other)
    with jax.named_scope("back"):
        error_out, q_factor = back(mine, f, c_own, c_other, inv, (u, *got))
    return momentum_out, error_out, p_factor, q_factor


def solution(mesh):
    fine = Mesh(mesh.devices.reshape(NZ, NX, NY, NC), ("z", "x", "y", "c"))
    dp, tensor = ("z", "x"), ("y", "c")
    big = P(dp, None, None, tensor)
    return jax.shard_map(
        local,
        mesh=fine,
        in_specs=(big, big, big, P(tensor, None)),
        out_specs=(big, big, P(), P(tensor, None)),
        check_vma=False,
    )
```

```python
import jax
import jax.numpy as jnp
from jax import lax
from jax.experimental import pallas as pl
from jax.experimental.pallas import tpu as pltpu
from jax.sharding import Mesh
from jax.sharding import PartitionSpec as P

BF, F32 = jnp.bfloat16, jnp.float32
NZ, NX, NY, NC = 8, 4, 4, 2
ROWS, COLS, RANK2 = 4096, 128, 128
HALF = ROWS // NC
BLK = HALF // (NX * NY)
FRONT, PROD, BACK = 1024, 512, 512
PANEL = 8
MIB = 1 << 20


def dot(a, b, dims=((1,), (0,)), precision=None):
    return lax.dot_general(a, b, (dims, ((), ())), precision=precision, preferred_element_type=F32)


def left_lanes(shape):
    return lax.broadcasted_iota(jnp.int32, shape, len(shape) - 1) < RANK2 // 2


def front_body(half_ref, g_hbm, m_hbm, e_hbm, q_hbm, mo_ref, c_ref, p_ref, g_buf, m_buf, e_buf, q_buf, sem, q_sem):
    base = pl.multiple_of(half_ref[0] * HALF, HALF)

    def loads(k):
        here = pl.ds(pl.multiple_of(k * FRONT, FRONT), FRONT)
        there = pl.ds(pl.multiple_of(base + k * FRONT, FRONT), FRONT)
        return [
            pltpu.make_async_copy(hbm.at[0, :, there], buf.at[:, here], sem.at[i, k])
            for i, (hbm, buf) in enumerate(((m_hbm, m_buf), (g_hbm, g_buf), (e_hbm, e_buf)))
        ]

    load_q = pltpu.make_async_copy(q_hbm, q_buf, q_sem)
    load_q.start()
    for k in range(HALF // FRONT):
        for copy in loads(k):
            copy.start()
    load_q.wait()
    q = q_buf[...]
    left = left_lanes(q.shape)
    q_of = [jnp.where(left if group == 0 else ~left, q, jnp.zeros_like(q)) for group in range(2)]

    for k in range(HALF // FRONT):
        for copy in loads(k):
            copy.wait()
        rows = pl.ds(pl.multiple_of(k * FRONT, FRONT), FRONT)
        total = None
        for group in range(2):
            mo = (0.9 * m_buf[group, rows].astype(F32) + g_buf[group, rows].astype(F32)).astype(BF)
            co = (mo.astype(F32) + e_buf[group, rows].astype(F32)).astype(BF)
            mo_ref[group, rows] = mo
            c_ref[group, rows] = co
            term = dot(co, q_of[group])
            total = term if total is None else total + term
        p_ref[rows] = total.astype(p_ref.dtype)


def front(half, args, p_dtype):
    hbm, vmem = pl.BlockSpec(memory_space=pltpu.HBM), pl.BlockSpec(memory_space=pltpu.VMEM)
    return pl.pallas_call(
        front_body,
        in_specs=[pl.BlockSpec(memory_space=pltpu.SMEM)] + [hbm] * 4,
        out_specs=[vmem] * 3,
        out_shape=[pltpu.VMEM((2, HALF, COLS), BF), pltpu.VMEM((2, HALF, COLS), BF), pltpu.VMEM((HALF, RANK2), p_dtype)],
        scratch_shapes=[pltpu.VMEM((2, HALF, COLS), BF)] * 3
        + [pltpu.VMEM((COLS, RANK2), BF), pltpu.SemaphoreType.DMA((3, HALF // FRONT)), pltpu.SemaphoreType.DMA],
        compiler_params=pltpu.CompilerParams(vmem_limit_bytes=16 * MIB),
        cost_estimate=pl.CostEstimate(flops=2 * HALF * 256 * 128, bytes_accessed=4 * MIB, transcendentals=0),
    )(half, *(pltpu.with_memory_space_constraint(x, pltpu.HBM) for x in args))


def sum_copies_body(x_ref, o_ref):
    total = x_ref[0].astype(F32)
    for k in range(1, x_ref.shape[0]):
        total = total + x_ref[k].astype(F32)
    total = total.astype(BF)
    for k in range(o_ref.shape[0]):
        o_ref[k] = total


def sum_copies(x, copies):
    return pl.pallas_call(
        sum_copies_body,
        out_shape=jax.ShapeDtypeStruct((copies, *x.shape[1:]), BF),
        compiler_params=pltpu.CompilerParams(vmem_limit_bytes=16 * MIB),
    )(x)


def products_body(p_ref, c_ref, *rest):
    u_ref, g_ref = rest[-2:]
    n = RANK2 // 2
    u0 = u1 = gram = None
    for k in range(HALF // PROD):
        rows = pl.ds(k * PROD, PROD)
        p = p_ref[rows]
        pt = p.T
        a, b, c = dot(pt[:n], c_ref[0, rows]), dot(pt[n:], c_ref[1, rows]), dot(pt, p)
        u0, u1, gram = (a, b, c) if u0 is None else (u0 + a, u1 + b, gram + c)
    u = jnp.concatenate([u0, u1], axis=0)
    if len(rest) == 2:
        u_ref[...] = u
        g_ref[...] = gram
    else:
        u_ref[...] = (u + rest[0][...]).astype(BF)
        g_ref[...] = gram + rest[1][...]


def products(p, c, before):
    last = before is not None
    return pl.pallas_call(
        products_body,
        out_shape=[
            jax.ShapeDtypeStruct((RANK2, COLS), BF if last else F32),
            jax.ShapeDtypeStruct((RANK2, RANK2), F32),
        ],
        compiler_params=pltpu.CompilerParams(vmem_limit_bytes=16 * MIB),
        cost_estimate=pl.CostEstimate(flops=2 * HALF * 256 * 128, bytes_accessed=2 * MIB, transcendentals=0),
    )(p, c, *(before if last else ()))


def invert(g_ref, o_ref):
    n, t = RANK2 // 2, PANEL
    tiles = n // t
    lane = lax.broadcasted_iota(jnp.int32, (t, 2 * n), 1)
    sub = lax.broadcasted_iota(jnp.int32, (t, 2 * n), 0)
    left = lane < n

    def spread(x):
        return jnp.broadcast_to(x, (t, 2 * n))

    both = []
    for s in range(2):
        for i in range(tiles):
            x = g_ref[s * n + t * i : s * n + t * i + t]
            x = pltpu.roll(x, n, 1) if s else x
            both.append(jnp.where(left, x, jnp.where(lane == sub + (t * i + n), 1.0, 0.0)))

    for top in range(tiles):
        first, live, out = top * t, tiles - top, []
        for s in range(2):
            a = list(both[s * live : (s + 1) * live])
            forward = full = a[0]
            c = [spread(full[:, first + j : first + j + 1]) for j in range(t)]
            pivots = None
            for j in range(t):
                d = spread(c[j][j : j + 1])
                pivots = d if j == 0 else jnp.where(sub == j, d, pivots)
                scale = 1.0 / d
                factor = c[j] * scale
                row = spread(forward[j : j + 1])
                full = jnp.where(sub == j, row * scale, full - factor * row)
                forward = forward - jnp.where(sub > j, factor, 0.0) * row
                for q in range(j + 1, t):
                    value = spread(c[j][q : q + 1])
                    c[q] = jnp.where(sub == j, value * scale, c[q] - factor * value)
            y = forward * lax.rsqrt(pivots)
            o_ref[pl.ds(s * n + first, t)] = jnp.where(left, 0.0, y) if s else jnp.where(left, pltpu.roll(y, n, 1), 0.0)
            solved = [spread(full[j : j + 1]) for j in range(t)]
            for x in a[1:]:
                columns = [spread(x[:, first + j : first + j + 1]) for j in range(t)]
                for j in range(t):
                    x = x - columns[j] * solved[j]
                out.append(x)
        both = out


def inverse_body(half_ref, g_ref, mo_ref, mt_ref, o_ref, m_hbm, sem):
    copies = []
    for i, ref in enumerate((mo_ref, mt_ref)):
        half = half_ref[0] if i == 0 else 1 - half_ref[0]
        there = pl.ds(pl.multiple_of(half * HALF, HALF), HALF)
        copies.append(pltpu.make_async_copy(ref, m_hbm.at[0, :, there], sem.at[i]))
        copies[-1].start()
    invert(g_ref, o_ref)
    for copy in copies:
        copy.wait()


def inverse(half, gram, mo_own, mo_other):
    vmem = pl.BlockSpec(memory_space=pltpu.VMEM)
    return pl.pallas_call(
        inverse_body,
        in_specs=[pl.BlockSpec(memory_space=pltpu.SMEM), vmem, vmem, vmem],
        out_specs=[vmem, pl.BlockSpec(memory_space=pltpu.HBM)],
        out_shape=[jax.ShapeDtypeStruct((RANK2, RANK2), F32), jax.ShapeDtypeStruct((1, 2, ROWS, COLS), BF)],
        scratch_shapes=[pltpu.SemaphoreType.DMA((2,))],
        compiler_params=pltpu.CompilerParams(vmem_limit_bytes=16 * MIB),
        cost_estimate=pl.CostEstimate(flops=64**3, bytes_accessed=6 * MIB, transcendentals=128),
    )(half, gram, mo_own, mo_other)


def factor_body(half_ref, l_ref, po_ref, pt_ref, p_hbm, f_ref, w_ref, sem):
    inv_t = l_ref[...].T
    hi = inv_t.astype(BF)
    w_ref[:RANK2] = hi
    w_ref[RANK2:] = (inv_t - hi.astype(F32)).astype(BF)
    weights = w_ref[...]
    moves = []
    for which, p_ref in enumerate((po_ref, pt_ref)):
        half = half_ref[0] if which == 0 else 1 - half_ref[0]
        for k in range(HALF // BACK):
            p = p_ref[pl.ds(k * BACK, BACK)]
            f_ref[pl.ds(which * HALF + k * BACK, BACK)] = dot(jnp.concatenate([p, p], axis=1), weights).astype(BF)
        there = pl.ds(pl.multiple_of(half * HALF, HALF), HALF)
        moves.append(pltpu.make_async_copy(f_ref.at[pl.ds(which * HALF, HALF)], p_hbm.at[there], sem.at[which]))
        moves[-1].start()
    for copy in moves:
        copy.wait()


def factor(half, inv, p_own, p_other):
    hbm, vmem = pl.BlockSpec(memory_space=pltpu.HBM), pl.BlockSpec(memory_space=pltpu.VMEM)
    return pl.pallas_call(
        factor_body,
        in_specs=[pl.BlockSpec(memory_space=pltpu.SMEM)] + [vmem] * 3,
        out_specs=[hbm, vmem],
        out_shape=[jax.ShapeDtypeStruct((ROWS, RANK2), BF), pltpu.VMEM((ROWS, RANK2), BF)],
        scratch_shapes=[pltpu.VMEM((2 * RANK2, RANK2), BF), pltpu.SemaphoreType.DMA((2,))],
        compiler_params=pltpu.CompilerParams(vmem_limit_bytes=16 * MIB),
        cost_estimate=pl.CostEstimate(flops=4 * ROWS * 128 * 128, bytes_accessed=6 * MIB, transcendentals=0),
    )(half, inv, p_own, p_other)


def back_body(half_ref, f_ref, co_ref, ct_ref, l_ref, u_ref, a_ref, b_ref, d_ref, e_hbm, q_ref, e_buf, w_ref, sem):
    u, a, b, d = (t[...].astype(F32) for t in (u_ref, a_ref, b_ref, d_ref))
    qt = dot(l_ref[...], (u + a) + (b + d), precision=lax.Precision.HIGHEST) * (1.0 / (NZ * NX))
    q_ref[...] = qt.T
    qt = qt.astype(BF)
    top = lax.broadcasted_iota(jnp.int32, qt.shape, 0) < RANK2 // 2
    zero = jnp.zeros_like(qt)
    w_ref[...] = jnp.concatenate([jnp.where(top, qt, zero), jnp.where(top, zero, qt)], axis=1)
    weights = w_ref[...]

    def store(which, k):
        half = half_ref[0] if which == 0 else 1 - half_ref[0]
        here = pl.ds(pl.multiple_of(which * HALF + k * BACK, BACK), BACK)
        there = pl.ds(pl.multiple_of(half * HALF + k * BACK, BACK), BACK)
        return here, pltpu.make_async_copy(e_buf.at[:, here], e_hbm.at[0, :, there], sem.at[which, k])

    for which, c_ref in enumerate((co_ref, ct_ref)):

        for k in range(HALF // BACK):
            here, copy = store(which, k)
            approx = dot(f_ref[here], weights)
            for group in range(2):
                c = c_ref[group, pl.ds(pl.multiple_of(k * BACK, BACK), BACK)].astype(F32)
                e_buf[group, here] = (c - approx[:, group * COLS : (group + 1) * COLS]).astype(BF)
            copy.start()

    for which in range(2):

        for k in range(HALF // BACK):
            store(which, k)[1].wait()


def back(half, f, c_own, c_other, inv, us):
    vmem = pl.BlockSpec(memory_space=pltpu.VMEM)
    return pl.pallas_call(
        back_body,
        in_specs=[pl.BlockSpec(memory_space=pltpu.SMEM)] + [vmem] * 8,
        out_specs=[pl.BlockSpec(memory_space=pltpu.HBM), vmem],
        out_shape=[
            jax.ShapeDtypeStruct((1, 2, ROWS, COLS), BF),
            jax.ShapeDtypeStruct((COLS, RANK2), F32),
        ],
        scratch_shapes=[
            pltpu.VMEM((2, ROWS, COLS), BF),
            pltpu.VMEM((RANK2, 2 * COLS), BF),
            pltpu.SemaphoreType.DMA((2, HALF // BACK)),
        ],
        compiler_params=pltpu.CompilerParams(vmem_limit_bytes=16 * MIB),
        cost_estimate=pl.CostEstimate(flops=4 * ROWS * 128 * 128, bytes_accessed=6 * MIB, transcendentals=0),
    )(half, f, c_own, c_other, inv, *us)


def swap_cores(x):
    return lax.ppermute(x, "c", [(0, 1), (1, 0)])


def pair(x, axis, size, flip):
    return lax.ppermute(x, axis, [(i, i ^ flip) for i in range(size)])


def plus(a, b):
    return (a.astype(F32) + b.astype(F32)).astype(BF)


def exchange(x, axes):
    return lax.all_to_all(x, axes, 0, 0)


def local(grads, momentum, error, q_warm):
    c = lax.axis_index("c").astype(jnp.int32)
    mine, theirs = c.reshape(1), (1 - c).reshape(1)

    with jax.named_scope("p_partial"):
        args = (grads, momentum, error, q_warm)
        mo_other, c_other, p_send = front(theirs, args, BF)
        p_got = swap_cores(p_send)
        mo_own, c_own, p_own = front(mine, args, F32)
        chip = (p_own + p_got.astype(F32)).astype(BF)
    with jax.named_scope("p_sum"):
        parts = exchange(chip.reshape(NX * NY, BLK, RANK2), ("x", "y"))
        parts = exchange(sum_copies(parts, NZ), "z")
        p_mine = exchange(sum_copies(parts, NX * NY), ("x", "y")).reshape(HALF, RANK2)
        p_theirs = swap_cores(p_mine)
    with jax.named_scope("u_sum"):
        first = products(p_mine, c_own, None)
        u, gram = products(p_theirs, c_other, first)
        got = pair(u, "z", NZ, 1)
        got, inv, momentum_out = lax.optimization_barrier((got, *inverse(mine, gram, mo_own, mo_other)))
        u = plus(u, got)
        got = pair(u, "z", NZ, 2)
        got, p_factor, f = lax.optimization_barrier((got, *factor(mine, inv, p_mine, p_theirs)))
        u = plus(u, got)
        u = plus(u, pair(u, "z", NZ, 6))
        got = [pair(u, "x", NX, k) for k in (1, 2, 3)]
    with jax.named_scope("back"):
        error_out, q_factor = back(mine, f, c_own, c_other, inv, (u, *got))
    return momentum_out, error_out, p_factor, q_factor


def solution(mesh):
    fine = Mesh(mesh.devices.reshape(NZ, NX, NY, NC), ("z", "x", "y", "c"))
    dp, tensor = ("z", "x"), ("y", "c")
    big = P(dp, None, None, tensor)
    return jax.shard_map(
        local,
        mesh=fine,
        in_specs=(big, big, big, P(tensor, None)),
        out_specs=(big, big, P(), P(tensor, None)),
        check_vma=False,
    )
```

```python
import jax
import jax.numpy as jnp
from jax import lax
from jax.experimental import pallas as pl
from jax.experimental.pallas import tpu as pltpu
from jax.sharding import Mesh
from jax.sharding import PartitionSpec as P

BF, F32 = jnp.bfloat16, jnp.float32
NZ, NX, NY, NC = 8, 4, 4, 2
ROWS, COLS, RANK2 = 4096, 128, 128
HALF = ROWS // NC
BLK = HALF // (NX * NY)
FRONT, PROD, BACK = 1024, 512, 256
PANEL = 8
MIB = 1 << 20


def dot(a, b, dims=((1,), (0,)), precision=None):
    return lax.dot_general(a, b, (dims, ((), ())), precision=precision, preferred_element_type=F32)


def left_lanes(shape):
    return lax.broadcasted_iota(jnp.int32, shape, len(shape) - 1) < RANK2 // 2


def front_body(half_ref, g_hbm, m_hbm, e_hbm, q_hbm, mo_ref, c_ref, p_ref, g_buf, m_buf, e_buf, q_buf, sem, q_sem):
    base = pl.multiple_of(half_ref[0] * HALF, HALF)

    def loads(k):
        here = pl.ds(pl.multiple_of(k * FRONT, FRONT), FRONT)
        there = pl.ds(pl.multiple_of(base + k * FRONT, FRONT), FRONT)
        return [
            pltpu.make_async_copy(hbm.at[0, :, there], buf.at[:, here], sem.at[i, k])
            for i, (hbm, buf) in enumerate(((m_hbm, m_buf), (g_hbm, g_buf), (e_hbm, e_buf)))
        ]

    load_q = pltpu.make_async_copy(q_hbm, q_buf, q_sem)
    load_q.start()
    for k in range(HALF // FRONT):
        for copy in loads(k):
            copy.start()
    load_q.wait()
    q = q_buf[...]
    left = left_lanes(q.shape)
    q_of = [jnp.where(left if group == 0 else ~left, q, jnp.zeros_like(q)) for group in range(2)]

    for k in range(HALF // FRONT):
        for copy in loads(k):
            copy.wait()
        rows = pl.ds(pl.multiple_of(k * FRONT, FRONT), FRONT)
        total = None
        for group in range(2):
            mo = (0.9 * m_buf[group, rows].astype(F32) + g_buf[group, rows].astype(F32)).astype(BF)
            co = (mo.astype(F32) + e_buf[group, rows].astype(F32)).astype(BF)
            mo_ref[group, rows] = mo
            c_ref[group, rows] = co
            term = dot(co, q_of[group])
            total = term if total is None else total + term
        p_ref[rows] = total.astype(p_ref.dtype)


def front(half, args, p_dtype):
    hbm, vmem = pl.BlockSpec(memory_space=pltpu.HBM), pl.BlockSpec(memory_space=pltpu.VMEM)
    return pl.pallas_call(
        front_body,
        in_specs=[pl.BlockSpec(memory_space=pltpu.SMEM)] + [hbm] * 4,
        out_specs=[vmem] * 3,
        out_shape=[pltpu.VMEM((2, HALF, COLS), BF), pltpu.VMEM((2, HALF, COLS), BF), pltpu.VMEM((HALF, RANK2), p_dtype)],
        scratch_shapes=[pltpu.VMEM((2, HALF, COLS), BF)] * 3
        + [pltpu.VMEM((COLS, RANK2), BF), pltpu.SemaphoreType.DMA((3, HALF // FRONT)), pltpu.SemaphoreType.DMA],
        compiler_params=pltpu.CompilerParams(vmem_limit_bytes=16 * MIB),
        cost_estimate=pl.CostEstimate(flops=2 * HALF * 256 * 128, bytes_accessed=4 * MIB, transcendentals=0),
    )(half, *(pltpu.with_memory_space_constraint(x, pltpu.HBM) for x in args))


def sum_copies_body(x_ref, o_ref):
    total = x_ref[0].astype(F32)
    for k in range(1, x_ref.shape[0]):
        total = total + x_ref[k].astype(F32)
    total = total.astype(BF)
    for k in range(o_ref.shape[0]):
        o_ref[k] = total


def sum_copies(x, copies):
    return pl.pallas_call(
        sum_copies_body,
        out_shape=jax.ShapeDtypeStruct((copies, *x.shape[1:]), BF),
        compiler_params=pltpu.CompilerParams(vmem_limit_bytes=16 * MIB),
    )(x)


def products_body(p_ref, c_ref, *rest):
    u_ref, g_ref = rest[-2:]
    n = RANK2 // 2
    u0 = u1 = gram = None
    for k in range(HALF // PROD):
        rows = pl.ds(k * PROD, PROD)
        p = p_ref[rows]
        pt = p.T
        a, b, c = dot(pt[:n], c_ref[0, rows]), dot(pt[n:], c_ref[1, rows]), dot(pt, p)
        u0, u1, gram = (a, b, c) if u0 is None else (u0 + a, u1 + b, gram + c)
    u = jnp.concatenate([u0, u1], axis=0)
    if len(rest) == 2:
        u_ref[...] = u
        g_ref[...] = gram
    else:
        u_ref[...] = (u + rest[0][...]).astype(BF)
        g_ref[...] = gram + rest[1][...]


def products(p, c, before):
    last = before is not None
    return pl.pallas_call(
        products_body,
        out_shape=[
            jax.ShapeDtypeStruct((RANK2, COLS), BF if last else F32),
            jax.ShapeDtypeStruct((RANK2, RANK2), F32),
        ],
        compiler_params=pltpu.CompilerParams(vmem_limit_bytes=16 * MIB),
        cost_estimate=pl.CostEstimate(flops=2 * HALF * 256 * 128, bytes_accessed=2 * MIB, transcendentals=0),
    )(p, c, *(before if last else ()))


def invert(g_ref, o_ref):
    n, t = RANK2 // 2, PANEL
    tiles = n // t
    lane = lax.broadcasted_iota(jnp.int32, (t, 2 * n), 1)
    sub = lax.broadcasted_iota(jnp.int32, (t, 2 * n), 0)
    left = lane < n

    def spread(x):
        return jnp.broadcast_to(x, (t, 2 * n))

    both = []
    for s in range(2):
        for i in range(tiles):
            x = g_ref[s * n + t * i : s * n + t * i + t]
            x = pltpu.roll(x, n, 1) if s else x
            both.append(jnp.where(left, x, jnp.where(lane == sub + (t * i + n), 1.0, 0.0)))

    for top in range(tiles):
        first, live, out = top * t, tiles - top, []
        for s in range(2):
            a = list(both[s * live : (s + 1) * live])
            forward = full = a[0]
            c = [spread(full[:, first + j : first + j + 1]) for j in range(t)]
            pivots = None
            for j in range(t):
                d = spread(c[j][j : j + 1])
                pivots = d if j == 0 else jnp.where(sub == j, d, pivots)
                scale = 1.0 / d
                factor = c[j] * scale
                row = spread(forward[j : j + 1])
                full = jnp.where(sub == j, row * scale, full - factor * row)
                forward = forward - jnp.where(sub > j, factor, 0.0) * row
                for q in range(j + 1, t):
                    value = spread(c[j][q : q + 1])
                    c[q] = jnp.where(sub == j, value * scale, c[q] - factor * value)
            y = forward * lax.rsqrt(pivots)
            o_ref[pl.ds(s * n + first, t)] = jnp.where(left, 0.0, y) if s else jnp.where(left, pltpu.roll(y, n, 1), 0.0)
            solved = [spread(full[j : j + 1]) for j in range(t)]
            for x in a[1:]:
                columns = [spread(x[:, first + j : first + j + 1]) for j in range(t)]
                for j in range(t):
                    x = x - columns[j] * solved[j]
                out.append(x)
        both = out


def inverse_body(half_ref, g_ref, mo_ref, mt_ref, o_ref, m_hbm, sem):
    copies = []
    for i, ref in enumerate((mo_ref, mt_ref)):
        half = half_ref[0] if i == 0 else 1 - half_ref[0]
        there = pl.ds(pl.multiple_of(half * HALF, HALF), HALF)
        copies.append(pltpu.make_async_copy(ref, m_hbm.at[0, :, there], sem.at[i]))
        copies[-1].start()
    invert(g_ref, o_ref)
    for copy in copies:
        copy.wait()


def inverse(half, gram, mo_own, mo_other):
    vmem = pl.BlockSpec(memory_space=pltpu.VMEM)
    return pl.pallas_call(
        inverse_body,
        in_specs=[pl.BlockSpec(memory_space=pltpu.SMEM), vmem, vmem, vmem],
        out_specs=[vmem, pl.BlockSpec(memory_space=pltpu.HBM)],
        out_shape=[jax.ShapeDtypeStruct((RANK2, RANK2), F32), jax.ShapeDtypeStruct((1, 2, ROWS, COLS), BF)],
        scratch_shapes=[pltpu.SemaphoreType.DMA((2,))],
        compiler_params=pltpu.CompilerParams(vmem_limit_bytes=16 * MIB),
        cost_estimate=pl.CostEstimate(flops=64**3, bytes_accessed=6 * MIB, transcendentals=128),
    )(half, gram, mo_own, mo_other)


def factor_body(half_ref, l_ref, po_ref, pt_ref, p_hbm, f_ref, w_ref, sem):
    inv_t = l_ref[...].T
    hi = inv_t.astype(BF)
    w_ref[:RANK2] = hi
    w_ref[RANK2:] = (inv_t - hi.astype(F32)).astype(BF)
    weights = w_ref[...]
    moves = []
    for which, p_ref in enumerate((po_ref, pt_ref)):
        half = half_ref[0] if which == 0 else 1 - half_ref[0]
        for k in range(HALF // BACK):
            p = p_ref[pl.ds(k * BACK, BACK)]
            f_ref[pl.ds(which * HALF + k * BACK, BACK)] = dot(jnp.concatenate([p, p], axis=1), weights).astype(BF)
        there = pl.ds(pl.multiple_of(half * HALF, HALF), HALF)
        moves.append(pltpu.make_async_copy(f_ref.at[pl.ds(which * HALF, HALF)], p_hbm.at[there], sem.at[which]))
        moves[-1].start()
    for copy in moves:
        copy.wait()


def factor(half, inv, p_own, p_other):
    hbm, vmem = pl.BlockSpec(memory_space=pltpu.HBM), pl.BlockSpec(memory_space=pltpu.VMEM)
    return pl.pallas_call(
        factor_body,
        in_specs=[pl.BlockSpec(memory_space=pltpu.SMEM)] + [vmem] * 3,
        out_specs=[hbm, vmem],
        out_shape=[jax.ShapeDtypeStruct((ROWS, RANK2), BF), pltpu.VMEM((ROWS, RANK2), BF)],
        scratch_shapes=[pltpu.VMEM((2 * RANK2, RANK2), BF), pltpu.SemaphoreType.DMA((2,))],
        compiler_params=pltpu.CompilerParams(vmem_limit_bytes=16 * MIB),
        cost_estimate=pl.CostEstimate(flops=4 * ROWS * 128 * 128, bytes_accessed=6 * MIB, transcendentals=0),
    )(half, inv, p_own, p_other)


def split(x):
    hi = x.astype(BF)
    return hi, (x - hi.astype(F32)).astype(BF)


def back_body(half_ref, f_ref, co_ref, ct_ref, l_ref, u_ref, a_ref, b_ref, d_ref, e_hbm, q_ref, e_buf, w_ref, sem):
    u, a, b, d = (t[...].astype(F32) for t in (u_ref, a_ref, b_ref, d_ref))
    (ih, il), (uh, ul) = split(l_ref[...]), split(((u + a) + (b + d)) * (1.0 / (NZ * NX)))
    qt = dot(jnp.concatenate([ih, il], axis=1), jnp.concatenate([uh, uh], axis=0)) + dot(ih, ul)
    q_ref[...] = qt
    qt = qt.astype(BF)
    top = lax.broadcasted_iota(jnp.int32, qt.shape, 0) < RANK2 // 2
    zero = jnp.zeros_like(qt)
    w_ref[...] = jnp.concatenate([jnp.where(top, qt, zero), jnp.where(top, zero, qt)], axis=1)
    weights = w_ref[...]
    copies = []
    for which, c_ref in enumerate((co_ref, ct_ref)):
        half = half_ref[0] if which == 0 else 1 - half_ref[0]
        for k in range(HALF // BACK):
            here = pl.ds(which * HALF + k * BACK, BACK)
            there = pl.ds(pl.multiple_of(half * HALF + k * BACK, BACK), BACK)
            approx = dot(f_ref[here], weights)
            for group in range(2):
                c = c_ref[group, pl.ds(k * BACK, BACK)].astype(F32)
                e_buf[group, here] = (c - approx[:, group * COLS : (group + 1) * COLS]).astype(BF)
            copies.append(pltpu.make_async_copy(e_buf.at[:, here], e_hbm.at[0, :, there], sem.at[which, k]))
            copies[-1].start()
    q_ref[...] = q_ref[...].T
    for copy in copies:
        copy.wait()


def back(half, f, c_own, c_other, inv, us):
    vmem = pl.BlockSpec(memory_space=pltpu.VMEM)
    return pl.pallas_call(
        back_body,
        in_specs=[pl.BlockSpec(memory_space=pltpu.SMEM)] + [vmem] * 8,
        out_specs=[pl.BlockSpec(memory_space=pltpu.HBM), vmem],
        out_shape=[
            jax.ShapeDtypeStruct((1, 2, ROWS, COLS), BF),
            jax.ShapeDtypeStruct((COLS, RANK2), F32),
        ],
        scratch_shapes=[
            pltpu.VMEM((2, ROWS, COLS), BF),
            pltpu.VMEM((RANK2, 2 * COLS), BF),
            pltpu.SemaphoreType.DMA((2, HALF // BACK)),
        ],
        compiler_params=pltpu.CompilerParams(vmem_limit_bytes=16 * MIB),
        cost_estimate=pl.CostEstimate(flops=4 * ROWS * 128 * 128, bytes_accessed=6 * MIB, transcendentals=0),
    )(half, f, c_own, c_other, inv, *us)


def swap_cores(x):
    return lax.ppermute(x, "c", [(0, 1), (1, 0)])


def pair(x, axis, size, flip):
    return lax.ppermute(x, axis, [(i, i ^ flip) for i in range(size)])


def plus(a, b):
    return (a.astype(F32) + b.astype(F32)).astype(BF)


def exchange(x, axes):
    return lax.all_to_all(x, axes, 0, 0)


def local(grads, momentum, error, q_warm):
    c = lax.axis_index("c").astype(jnp.int32)
    mine, theirs = c.reshape(1), (1 - c).reshape(1)

    with jax.named_scope("p_partial"):
        args = (grads, momentum, error, q_warm)
        mo_other, c_other, p_send = front(theirs, args, BF)
        p_got = swap_cores(p_send)
        mo_own, c_own, p_own = front(mine, args, F32)
        chip = (p_own + p_got.astype(F32)).astype(BF)
    with jax.named_scope("p_sum"):
        parts = exchange(chip.reshape(NX * NY, BLK, RANK2), ("x", "y"))
        parts = exchange(sum_copies(parts, NZ), "z")
        p_mine = exchange(sum_copies(parts, NX * NY), ("x", "y")).reshape(HALF, RANK2)
        p_theirs = swap_cores(p_mine)
    with jax.named_scope("u_sum"):
        first = products(p_mine, c_own, None)
        u, gram = products(p_theirs, c_other, first)
        def tree(u, got):
            u, a, b, d = (t.astype(F32) for t in (u, *got))
            return ((u + a) + (b + d)).astype(BF)

        got = [pair(u, "z", NZ, k) for k in (1, 2, 3)]
        got, inv, momentum_out = lax.optimization_barrier((got, *inverse(mine, gram, mo_own, mo_other)))
        u = tree(u, got)
        got = pair(u, "z", NZ, 6)
        got, p_factor, f = lax.optimization_barrier((got, *factor(mine, inv, p_mine, p_theirs)))
        u = plus(u, got)
        got = [pair(u, "x", NX, k) for k in (1, 2, 3)]
    with jax.named_scope("back"):
        error_out, q_factor = back(mine, f, c_own, c_other, inv, (u, *got))
    return momentum_out, error_out, p_factor, q_factor


def solution(mesh):
    fine = Mesh(mesh.devices.reshape(NZ, NX, NY, NC), ("z", "x", "y", "c"))
    dp, tensor = ("z", "x"), ("y", "c")
    big = P(dp, None, None, tensor)
    return jax.shard_map(
        local,
        mesh=fine,
        in_specs=(big, big, big, P(tensor, None)),
        out_specs=(big, big, P(), P(tensor, None)),
        check_vma=False,
    )
```

```python
import jax
import jax.numpy as jnp
from jax import lax
from jax.experimental import pallas as pl
from jax.experimental.pallas import tpu as pltpu
from jax.sharding import Mesh
from jax.sharding import PartitionSpec as P

BF, F32 = jnp.bfloat16, jnp.float32
NZ, NX, NY, NC = 8, 4, 4, 2
ROWS, COLS, RANK2 = 4096, 128, 128
HALF = ROWS // NC
BLK = HALF // (NX * NY)
FRONT, PROD, BACK = 1024, 512, 256
PANEL = 8
MIB = 1 << 20


def dot(a, b, dims=((1,), (0,)), precision=None):
    return lax.dot_general(a, b, (dims, ((), ())), precision=precision, preferred_element_type=F32)


def left_lanes(shape):
    return lax.broadcasted_iota(jnp.int32, shape, len(shape) - 1) < RANK2 // 2


def front_body(half_ref, g_hbm, m_hbm, e_hbm, q_hbm, mo_ref, c_ref, p_ref, g_buf, m_buf, e_buf, q_buf, sem, q_sem):
    base = pl.multiple_of(half_ref[0] * HALF, HALF)

    def loads(k):
        here = pl.ds(pl.multiple_of(k * FRONT, FRONT), FRONT)
        there = pl.ds(pl.multiple_of(base + k * FRONT, FRONT), FRONT)
        return [
            pltpu.make_async_copy(hbm.at[0, :, there], buf.at[:, here], sem.at[i, k])
            for i, (hbm, buf) in enumerate(((m_hbm, m_buf), (g_hbm, g_buf), (e_hbm, e_buf)))
        ]

    load_q = pltpu.make_async_copy(q_hbm, q_buf, q_sem)
    load_q.start()
    for k in range(HALF // FRONT):
        for copy in loads(k):
            copy.start()
    load_q.wait()
    q = q_buf[...]
    left = left_lanes(q.shape)
    q_of = [jnp.where(left if group == 0 else ~left, q, jnp.zeros_like(q)) for group in range(2)]

    for k in range(HALF // FRONT):
        for copy in loads(k):
            copy.wait()
        rows = pl.ds(pl.multiple_of(k * FRONT, FRONT), FRONT)
        total = None
        for group in range(2):
            mo = (0.9 * m_buf[group, rows].astype(F32) + g_buf[group, rows].astype(F32)).astype(BF)
            co = (mo.astype(F32) + e_buf[group, rows].astype(F32)).astype(BF)
            mo_ref[group, rows] = mo
            c_ref[group, rows] = co
            term = dot(co, q_of[group])
            total = term if total is None else total + term
        p_ref[rows] = total.astype(p_ref.dtype)


def front(half, args, p_dtype):
    hbm, vmem = pl.BlockSpec(memory_space=pltpu.HBM), pl.BlockSpec(memory_space=pltpu.VMEM)
    return pl.pallas_call(
        front_body,
        in_specs=[pl.BlockSpec(memory_space=pltpu.SMEM)] + [hbm] * 4,
        out_specs=[vmem] * 3,
        out_shape=[pltpu.VMEM((2, HALF, COLS), BF), pltpu.VMEM((2, HALF, COLS), BF), pltpu.VMEM((HALF, RANK2), p_dtype)],
        scratch_shapes=[pltpu.VMEM((2, HALF, COLS), BF)] * 3
        + [pltpu.VMEM((COLS, RANK2), BF), pltpu.SemaphoreType.DMA((3, HALF // FRONT)), pltpu.SemaphoreType.DMA],
        compiler_params=pltpu.CompilerParams(vmem_limit_bytes=16 * MIB),
        cost_estimate=pl.CostEstimate(flops=2 * HALF * 256 * 128, bytes_accessed=4 * MIB, transcendentals=0),
    )(half, *(pltpu.with_memory_space_constraint(x, pltpu.HBM) for x in args))


def sum_copies_body(x_ref, o_ref):
    total = x_ref[0].astype(F32)
    for k in range(1, x_ref.shape[0]):
        total = total + x_ref[k].astype(F32)
    total = total.astype(BF)
    for k in range(o_ref.shape[0]):
        o_ref[k] = total


def sum_copies(x, copies):
    return pl.pallas_call(
        sum_copies_body,
        out_shape=jax.ShapeDtypeStruct((copies, *x.shape[1:]), BF),
        compiler_params=pltpu.CompilerParams(vmem_limit_bytes=16 * MIB),
    )(x)


def products_body(p_ref, c_ref, *rest):
    u_ref, g_ref = rest[-2:]
    n = RANK2 // 2
    u0 = u1 = gram = None
    for k in range(HALF // PROD):
        rows = pl.ds(k * PROD, PROD)
        p = p_ref[rows]
        pt = p.T
        a, b, c = dot(pt[:n], c_ref[0, rows]), dot(pt[n:], c_ref[1, rows]), dot(pt, p)
        u0, u1, gram = (a, b, c) if u0 is None else (u0 + a, u1 + b, gram + c)
    u = jnp.concatenate([u0, u1], axis=0)
    if len(rest) == 2:
        u_ref[...] = u
        g_ref[...] = gram
    else:
        u_ref[...] = (u + rest[0][...]).astype(BF)
        g_ref[...] = gram + rest[1][...]


def products(p, c, before):
    last = before is not None
    return pl.pallas_call(
        products_body,
        out_shape=[
            jax.ShapeDtypeStruct((RANK2, COLS), BF if last else F32),
            jax.ShapeDtypeStruct((RANK2, RANK2), F32),
        ],
        compiler_params=pltpu.CompilerParams(vmem_limit_bytes=16 * MIB),
        cost_estimate=pl.CostEstimate(flops=2 * HALF * 256 * 128, bytes_accessed=2 * MIB, transcendentals=0),
    )(p, c, *(before if last else ()))


def invert(g_ref, o_ref):
    n, t = RANK2 // 2, PANEL
    tiles = n // t
    lane = lax.broadcasted_iota(jnp.int32, (t, 2 * n), 1)
    sub = lax.broadcasted_iota(jnp.int32, (t, 2 * n), 0)
    left = lane < n

    def spread(x):
        return jnp.broadcast_to(x, (t, 2 * n))

    both = []
    for s in range(2):
        for i in range(tiles):
            x = g_ref[s * n + t * i : s * n + t * i + t]
            x = pltpu.roll(x, n, 1) if s else x
            both.append(jnp.where(left, x, jnp.where(lane == sub + (t * i + n), 1.0, 0.0)))

    for top in range(tiles):
        first, live, out = top * t, tiles - top, []
        for s in range(2):
            a = list(both[s * live : (s + 1) * live])
            forward = full = a[0]
            c = [spread(full[:, first + j : first + j + 1]) for j in range(t)]
            pivots = None
            for j in range(t):
                d = spread(c[j][j : j + 1])
                pivots = d if j == 0 else jnp.where(sub == j, d, pivots)
                scale = 1.0 / d
                factor = c[j] * scale
                row = spread(forward[j : j + 1])
                full = jnp.where(sub == j, row * scale, full - factor * row)
                forward = forward - jnp.where(sub > j, factor, 0.0) * row
                for q in range(j + 1, t):
                    value = spread(c[j][q : q + 1])
                    c[q] = jnp.where(sub == j, value * scale, c[q] - factor * value)
            y = forward * lax.rsqrt(pivots)
            o_ref[pl.ds(s * n + first, t)] = jnp.where(left, 0.0, y) if s else jnp.where(left, pltpu.roll(y, n, 1), 0.0)
            solved = [spread(full[j : j + 1]) for j in range(t)]
            for x in a[1:]:
                columns = [spread(x[:, first + j : first + j + 1]) for j in range(t)]
                for j in range(t):
                    x = x - columns[j] * solved[j]
                out.append(x)
        both = out


def inverse_body(half_ref, g_ref, mo_ref, mt_ref, o_ref, m_hbm, sem):
    copies = []
    for i, ref in enumerate((mo_ref, mt_ref)):
        half = half_ref[0] if i == 0 else 1 - half_ref[0]
        there = pl.ds(pl.multiple_of(half * HALF, HALF), HALF)
        copies.append(pltpu.make_async_copy(ref, m_hbm.at[0, :, there], sem.at[i]))
        copies[-1].start()
    invert(g_ref, o_ref)
    for copy in copies:
        copy.wait()


def inverse(half, gram, mo_own, mo_other):
    vmem = pl.BlockSpec(memory_space=pltpu.VMEM)
    return pl.pallas_call(
        inverse_body,
        in_specs=[pl.BlockSpec(memory_space=pltpu.SMEM), vmem, vmem, vmem],
        out_specs=[vmem, pl.BlockSpec(memory_space=pltpu.HBM)],
        out_shape=[jax.ShapeDtypeStruct((RANK2, RANK2), F32), jax.ShapeDtypeStruct((1, 2, ROWS, COLS), BF)],
        scratch_shapes=[pltpu.SemaphoreType.DMA((2,))],
        compiler_params=pltpu.CompilerParams(vmem_limit_bytes=16 * MIB),
        cost_estimate=pl.CostEstimate(flops=64**3, bytes_accessed=6 * MIB, transcendentals=128),
    )(half, gram, mo_own, mo_other)


def factor_body(half_ref, l_ref, po_ref, pt_ref, p_hbm, f_ref, w_ref, sem):
    inv_t = l_ref[...].T
    hi = inv_t.astype(BF)
    w_ref[:RANK2] = hi
    w_ref[RANK2:] = (inv_t - hi.astype(F32)).astype(BF)
    weights = w_ref[...]
    moves = []
    for which, p_ref in enumerate((po_ref, pt_ref)):
        half = half_ref[0] if which == 0 else 1 - half_ref[0]
        for k in range(HALF // BACK):
            p = p_ref[pl.ds(k * BACK, BACK)]
            f_ref[pl.ds(which * HALF + k * BACK, BACK)] = dot(jnp.concatenate([p, p], axis=1), weights).astype(BF)
        there = pl.ds(pl.multiple_of(half * HALF, HALF), HALF)
        moves.append(pltpu.make_async_copy(f_ref.at[pl.ds(which * HALF, HALF)], p_hbm.at[there], sem.at[which]))
        moves[-1].start()
    for copy in moves:
        copy.wait()


def factor(half, inv, p_own, p_other):
    hbm, vmem = pl.BlockSpec(memory_space=pltpu.HBM), pl.BlockSpec(memory_space=pltpu.VMEM)
    return pl.pallas_call(
        factor_body,
        in_specs=[pl.BlockSpec(memory_space=pltpu.SMEM)] + [vmem] * 3,
        out_specs=[hbm, vmem],
        out_shape=[jax.ShapeDtypeStruct((ROWS, RANK2), BF), pltpu.VMEM((ROWS, RANK2), BF)],
        scratch_shapes=[pltpu.VMEM((2 * RANK2, RANK2), BF), pltpu.SemaphoreType.DMA((2,))],
        compiler_params=pltpu.CompilerParams(vmem_limit_bytes=16 * MIB),
        cost_estimate=pl.CostEstimate(flops=4 * ROWS * 128 * 128, bytes_accessed=6 * MIB, transcendentals=0),
    )(half, inv, p_own, p_other)


def split(x):
    hi = x.astype(BF)
    return hi, (x - hi.astype(F32)).astype(BF)


def back_body(half_ref, f_ref, co_ref, ct_ref, l_ref, u_ref, a_ref, b_ref, d_ref, e_hbm, q_ref, e_buf, w_ref, sem):
    u, a, b, d = (t[...].astype(F32) for t in (u_ref, a_ref, b_ref, d_ref))
    (ih, il), (uh, ul) = split(l_ref[...]), split(((u + a) + (b + d)) * (1.0 / (NZ * NX)))
    qt = dot(jnp.concatenate([ih, il], axis=1), jnp.concatenate([uh, uh], axis=0)) + dot(ih, ul)
    q_ref[...] = qt
    qt = qt.astype(BF)
    top = lax.broadcasted_iota(jnp.int32, qt.shape, 0) < RANK2 // 2
    zero = jnp.zeros_like(qt)
    w_ref[...] = jnp.concatenate([jnp.where(top, qt, zero), jnp.where(top, zero, qt)], axis=1)
    weights = w_ref[...]
    copies = []
    for which, c_ref in enumerate((co_ref, ct_ref)):
        half = half_ref[0] if which == 0 else 1 - half_ref[0]
        for k in range(HALF // BACK):
            here = pl.ds(which * HALF + k * BACK, BACK)
            there = pl.ds(pl.multiple_of(half * HALF + k * BACK, BACK), BACK)
            approx = dot(f_ref[here], weights)
            for group in range(2):
                c = c_ref[group, pl.ds(k * BACK, BACK)].astype(F32)
                e_buf[group, here] = (c - approx[:, group * COLS : (group + 1) * COLS]).astype(BF)
            copies.append(pltpu.make_async_copy(e_buf.at[:, here], e_hbm.at[0, :, there], sem.at[which, k]))
            copies[-1].start()
    q_ref[...] = q_ref[...].T
    for copy in copies:
        copy.wait()


def back(half, f, c_own, c_other, inv, us):
    vmem = pl.BlockSpec(memory_space=pltpu.VMEM)
    return pl.pallas_call(
        back_body,
        in_specs=[pl.BlockSpec(memory_space=pltpu.SMEM)] + [vmem] * 8,
        out_specs=[pl.BlockSpec(memory_space=pltpu.HBM), vmem],
        out_shape=[
            jax.ShapeDtypeStruct((1, 2, ROWS, COLS), BF),
            jax.ShapeDtypeStruct((COLS, RANK2), F32),
        ],
        scratch_shapes=[
            pltpu.VMEM((2, ROWS, COLS), BF),
            pltpu.VMEM((RANK2, 2 * COLS), BF),
            pltpu.SemaphoreType.DMA((2, HALF // BACK)),
        ],
        compiler_params=pltpu.CompilerParams(vmem_limit_bytes=16 * MIB),
        cost_estimate=pl.CostEstimate(flops=4 * ROWS * 128 * 128, bytes_accessed=6 * MIB, transcendentals=0),
    )(half, f, c_own, c_other, inv, *us)


def swap_cores(x):
    return lax.ppermute(x, "c", [(0, 1), (1, 0)])


def pair(x, axis, size, flip):
    return lax.ppermute(x, axis, [(i, i ^ flip) for i in range(size)])


def plus(a, b):
    return (a.astype(F32) + b.astype(F32)).astype(BF)


def exchange(x, axes):
    return lax.all_to_all(x, axes, 0, 0)


def local(grads, momentum, error, q_warm):
    c = lax.axis_index("c").astype(jnp.int32)
    mine, theirs = c.reshape(1), (1 - c).reshape(1)

    with jax.named_scope("p_partial"):
        args = (grads, momentum, error, q_warm)
        mo_other, c_other, p_send = front(theirs, args, BF)
        p_got = swap_cores(p_send)
        mo_own, c_own, p_own = front(mine, args, F32)
        chip = (p_own + p_got.astype(F32)).astype(BF)
    with jax.named_scope("p_sum"):
        parts = exchange(chip.reshape(NX * NY, BLK, RANK2), ("x", "y"))
        parts = exchange(sum_copies(parts, NZ), "z")
        p_mine = exchange(sum_copies(parts, NX * NY), ("x", "y")).reshape(HALF, RANK2)
        p_theirs = swap_cores(p_mine)
    with jax.named_scope("u_sum"):
        first = products(p_mine, c_own, None)
        u, gram = products(p_theirs, c_other, first)
        def tree(u, got):
            u, a, b, d = (t.astype(F32) for t in (u, *got))
            return ((u + a) + (b + d)).astype(BF)

        got = pair(u, "z", NZ, 6)
        got, inv, momentum_out = lax.optimization_barrier((got, *inverse(mine, gram, mo_own, mo_other)))
        u = plus(u, got)
        got = [pair(u, "z", NZ, k) for k in (1, 2, 3)]
        got, p_factor, f = lax.optimization_barrier((got, *factor(mine, inv, p_mine, p_theirs)))
        u = tree(u, got)
        got = [pair(u, "x", NX, k) for k in (1, 2, 3)]
    with jax.named_scope("back"):
        error_out, q_factor = back(mine, f, c_own, c_other, inv, (u, *got))
    return momentum_out, error_out, p_factor, q_factor


def solution(mesh):
    fine = Mesh(mesh.devices.reshape(NZ, NX, NY, NC), ("z", "x", "y", "c"))
    dp, tensor = ("z", "x"), ("y", "c")
    big = P(dp, None, None, tensor)
    return jax.shard_map(
        local,
        mesh=fine,
        in_specs=(big, big, big, P(tensor, None)),
        out_specs=(big, big, P(), P(tensor, None)),
        check_vma=False,
    )
```

```python
import jax
import jax.numpy as jnp
from jax import lax
from jax.experimental import pallas as pl
from jax.experimental.pallas import tpu as pltpu
from jax.sharding import Mesh
from jax.sharding import PartitionSpec as P

BF, F32 = jnp.bfloat16, jnp.float32
NZ, NX, NY, NC = 8, 4, 4, 2
ROWS, COLS, RANK2 = 4096, 128, 128
HALF = ROWS // NC
BLK = HALF // (NX * NY)
FRONT, PROD, BACK = 1024, 512, 256
PANEL = 8
MIB = 1 << 20


def dot(a, b, dims=((1,), (0,)), precision=None):
    return lax.dot_general(a, b, (dims, ((), ())), precision=precision, preferred_element_type=F32)


def left_lanes(shape):
    return lax.broadcasted_iota(jnp.int32, shape, len(shape) - 1) < RANK2 // 2


def front_body(half_ref, g_hbm, m_hbm, e_hbm, q_hbm, mo_ref, c_ref, p_ref, g_buf, m_buf, e_buf, q_buf, sem, q_sem):
    base = pl.multiple_of(half_ref[0] * HALF, HALF)

    def loads(k):
        here = pl.ds(pl.multiple_of(k * FRONT, FRONT), FRONT)
        there = pl.ds(pl.multiple_of(base + k * FRONT, FRONT), FRONT)
        return [
            pltpu.make_async_copy(hbm.at[0, :, there], buf.at[:, here], sem.at[i, k])
            for i, (hbm, buf) in enumerate(((m_hbm, m_buf), (g_hbm, g_buf), (e_hbm, e_buf)))
        ]

    load_q = pltpu.make_async_copy(q_hbm, q_buf, q_sem)
    load_q.start()
    for k in range(HALF // FRONT):
        for copy in loads(k):
            copy.start()
    load_q.wait()
    q = q_buf[...]
    left = left_lanes(q.shape)
    q_of = [jnp.where(left if group == 0 else ~left, q, jnp.zeros_like(q)) for group in range(2)]

    for k in range(HALF // FRONT):
        for copy in loads(k):
            copy.wait()
        rows = pl.ds(pl.multiple_of(k * FRONT, FRONT), FRONT)
        total = None
        for group in range(2):
            mo = (0.9 * m_buf[group, rows].astype(F32) + g_buf[group, rows].astype(F32)).astype(BF)
            co = (mo.astype(F32) + e_buf[group, rows].astype(F32)).astype(BF)
            mo_ref[group, rows] = mo
            c_ref[group, rows] = co
            term = dot(co, q_of[group])
            total = term if total is None else total + term
        p_ref[rows] = total.astype(p_ref.dtype)


def front(half, args, p_dtype):
    hbm, vmem = pl.BlockSpec(memory_space=pltpu.HBM), pl.BlockSpec(memory_space=pltpu.VMEM)
    return pl.pallas_call(
        front_body,
        in_specs=[pl.BlockSpec(memory_space=pltpu.SMEM)] + [hbm] * 4,
        out_specs=[vmem] * 3,
        out_shape=[pltpu.VMEM((2, HALF, COLS), BF), pltpu.VMEM((2, HALF, COLS), BF), pltpu.VMEM((HALF, RANK2), p_dtype)],
        scratch_shapes=[pltpu.VMEM((2, HALF, COLS), BF)] * 3
        + [pltpu.VMEM((COLS, RANK2), BF), pltpu.SemaphoreType.DMA((3, HALF // FRONT)), pltpu.SemaphoreType.DMA],
        compiler_params=pltpu.CompilerParams(vmem_limit_bytes=16 * MIB),
        cost_estimate=pl.CostEstimate(flops=2 * HALF * 256 * 128, bytes_accessed=4 * MIB, transcendentals=0),
    )(half, *(pltpu.with_memory_space_constraint(x, pltpu.HBM) for x in args))


def sum_copies_body(x_ref, o_ref):
    terms = [x_ref[k].astype(F32) for k in range(x_ref.shape[0])]
    while len(terms) > 1:
        terms = [a + b for a, b in zip(terms[::2], terms[1::2])]
    total = terms[0].astype(BF)
    for k in range(o_ref.shape[0]):
        o_ref[k] = total


def sum_copies(x, copies):
    return pl.pallas_call(
        sum_copies_body,
        out_shape=jax.ShapeDtypeStruct((copies, *x.shape[1:]), BF),
        compiler_params=pltpu.CompilerParams(vmem_limit_bytes=16 * MIB),
    )(x)


def products_body(p_ref, c_ref, *rest):
    u_ref, g_ref = rest[-2:]
    n = RANK2 // 2
    u0 = u1 = gram = None
    for k in range(HALF // PROD):
        rows = pl.ds(k * PROD, PROD)
        p = p_ref[rows]
        pt = p.T
        a, b, c = dot(pt[:n], c_ref[0, rows]), dot(pt[n:], c_ref[1, rows]), dot(pt, p)
        u0, u1, gram = (a, b, c) if u0 is None else (u0 + a, u1 + b, gram + c)
    u = jnp.concatenate([u0, u1], axis=0)
    if len(rest) == 2:
        u_ref[...] = u
        g_ref[...] = gram
    else:
        u_ref[...] = (u + rest[0][...]).astype(BF)
        g_ref[...] = gram + rest[1][...]


def products(p, c, before):
    last = before is not None
    return pl.pallas_call(
        products_body,
        out_shape=[
            jax.ShapeDtypeStruct((RANK2, COLS), BF if last else F32),
            jax.ShapeDtypeStruct((RANK2, RANK2), F32),
        ],
        compiler_params=pltpu.CompilerParams(vmem_limit_bytes=16 * MIB),
        cost_estimate=pl.CostEstimate(flops=2 * HALF * 256 * 128, bytes_accessed=2 * MIB, transcendentals=0),
    )(p, c, *(before if last else ()))


def invert(g_ref, o_ref):
    n, t = RANK2 // 2, PANEL
    tiles = n // t
    lane = lax.broadcasted_iota(jnp.int32, (t, 2 * n), 1)
    sub = lax.broadcasted_iota(jnp.int32, (t, 2 * n), 0)
    left = lane < n

    def spread(x):
        return jnp.broadcast_to(x, (t, 2 * n))

    both = []
    for s in range(2):
        for i in range(tiles):
            x = g_ref[s * n + t * i : s * n + t * i + t]
            x = pltpu.roll(x, n, 1) if s else x
            both.append(jnp.where(left, x, jnp.where(lane == sub + (t * i + n), 1.0, 0.0)))

    for top in range(tiles):
        first, live, out = top * t, tiles - top, []
        for s in range(2):
            a = list(both[s * live : (s + 1) * live])
            forward = full = a[0]
            c = [spread(full[:, first + j : first + j + 1]) for j in range(t)]
            pivots = None
            for j in range(t):
                d = spread(c[j][j : j + 1])
                pivots = d if j == 0 else jnp.where(sub == j, d, pivots)
                scale = 1.0 / d
                factor = c[j] * scale
                row = spread(forward[j : j + 1])
                full = jnp.where(sub == j, row * scale, full - factor * row)
                forward = forward - jnp.where(sub > j, factor, 0.0) * row
                for q in range(j + 1, t):
                    value = spread(c[j][q : q + 1])
                    c[q] = jnp.where(sub == j, value * scale, c[q] - factor * value)
            y = forward * lax.rsqrt(pivots)
            o_ref[pl.ds(s * n + first, t)] = jnp.where(left, 0.0, y) if s else jnp.where(left, pltpu.roll(y, n, 1), 0.0)
            solved = [spread(full[j : j + 1]) for j in range(t)]
            for x in a[1:]:
                columns = [spread(x[:, first + j : first + j + 1]) for j in range(t)]
                for j in range(t):
                    x = x - columns[j] * solved[j]
                out.append(x)
        both = out


def inverse_body(half_ref, g_ref, mo_ref, mt_ref, o_ref, m_hbm, sem):
    copies = []
    for i, ref in enumerate((mo_ref, mt_ref)):
        half = half_ref[0] if i == 0 else 1 - half_ref[0]
        there = pl.ds(pl.multiple_of(half * HALF, HALF), HALF)
        copies.append(pltpu.make_async_copy(ref, m_hbm.at[0, :, there], sem.at[i]))
        copies[-1].start()
    invert(g_ref, o_ref)
    for copy in copies:
        copy.wait()


def inverse(half, gram, mo_own, mo_other):
    vmem = pl.BlockSpec(memory_space=pltpu.VMEM)
    return pl.pallas_call(
        inverse_body,
        in_specs=[pl.BlockSpec(memory_space=pltpu.SMEM), vmem, vmem, vmem],
        out_specs=[vmem, pl.BlockSpec(memory_space=pltpu.HBM)],
        out_shape=[jax.ShapeDtypeStruct((RANK2, RANK2), F32), jax.ShapeDtypeStruct((1, 2, ROWS, COLS), BF)],
        scratch_shapes=[pltpu.SemaphoreType.DMA((2,))],
        compiler_params=pltpu.CompilerParams(vmem_limit_bytes=16 * MIB),
        cost_estimate=pl.CostEstimate(flops=64**3, bytes_accessed=6 * MIB, transcendentals=128),
    )(half, gram, mo_own, mo_other)


def factor_body(half_ref, l_ref, po_ref, pt_ref, p_hbm, f_ref, w_ref, sem):
    inv_t = l_ref[...].T
    hi = inv_t.astype(BF)
    w_ref[:RANK2] = hi
    w_ref[RANK2:] = (inv_t - hi.astype(F32)).astype(BF)
    weights = w_ref[...]
    moves = []
    for which, p_ref in enumerate((po_ref, pt_ref)):
        half = half_ref[0] if which == 0 else 1 - half_ref[0]
        for k in range(HALF // BACK):
            p = p_ref[pl.ds(k * BACK, BACK)]
            f_ref[pl.ds(which * HALF + k * BACK, BACK)] = dot(jnp.concatenate([p, p], axis=1), weights).astype(BF)
        there = pl.ds(pl.multiple_of(half * HALF, HALF), HALF)
        moves.append(pltpu.make_async_copy(f_ref.at[pl.ds(which * HALF, HALF)], p_hbm.at[there], sem.at[which]))
        moves[-1].start()
    for copy in moves:
        copy.wait()


def factor(half, inv, p_own, p_other):
    hbm, vmem = pl.BlockSpec(memory_space=pltpu.HBM), pl.BlockSpec(memory_space=pltpu.VMEM)
    return pl.pallas_call(
        factor_body,
        in_specs=[pl.BlockSpec(memory_space=pltpu.SMEM)] + [vmem] * 3,
        out_specs=[hbm, vmem],
        out_shape=[jax.ShapeDtypeStruct((ROWS, RANK2), BF), pltpu.VMEM((ROWS, RANK2), BF)],
        scratch_shapes=[pltpu.VMEM((2 * RANK2, RANK2), BF), pltpu.SemaphoreType.DMA((2,))],
        compiler_params=pltpu.CompilerParams(vmem_limit_bytes=16 * MIB),
        cost_estimate=pl.CostEstimate(flops=4 * ROWS * 128 * 128, bytes_accessed=6 * MIB, transcendentals=0),
    )(half, inv, p_own, p_other)


def split(x):
    hi = x.astype(BF)
    return hi, (x - hi.astype(F32)).astype(BF)


def back_body(half_ref, f_ref, co_ref, ct_ref, l_ref, u_ref, a_ref, b_ref, d_ref, e_hbm, q_ref, e_buf, w_ref, sem):
    u, a, b, d = (t[...].astype(F32) for t in (u_ref, a_ref, b_ref, d_ref))
    (ih, il), (uh, ul) = split(l_ref[...]), split(((u + a) + (b + d)) * (1.0 / (NZ * NX)))
    qt = dot(jnp.concatenate([ih, il], axis=1), jnp.concatenate([uh, uh], axis=0)) + dot(ih, ul)
    q_ref[...] = qt
    qt = qt.astype(BF)
    top = lax.broadcasted_iota(jnp.int32, qt.shape, 0) < RANK2 // 2
    zero = jnp.zeros_like(qt)
    w_ref[...] = jnp.concatenate([jnp.where(top, qt, zero), jnp.where(top, zero, qt)], axis=1)
    weights = w_ref[...]
    copies = []
    for which, c_ref in enumerate((co_ref, ct_ref)):
        half = half_ref[0] if which == 0 else 1 - half_ref[0]
        for k in range(HALF // BACK):
            here = pl.ds(which * HALF + k * BACK, BACK)
            there = pl.ds(pl.multiple_of(half * HALF + k * BACK, BACK), BACK)
            approx = dot(f_ref[here], weights)
            for group in range(2):
                c = c_ref[group, pl.ds(k * BACK, BACK)].astype(F32)
                e_buf[group, here] = (c - approx[:, group * COLS : (group + 1) * COLS]).astype(BF)
            copies.append(pltpu.make_async_copy(e_buf.at[:, here], e_hbm.at[0, :, there], sem.at[which, k]))
            copies[-1].start()
    q_ref[...] = q_ref[...].T
    for copy in copies:
        copy.wait()


def back(half, f, c_own, c_other, inv, us):
    vmem = pl.BlockSpec(memory_space=pltpu.VMEM)
    return pl.pallas_call(
        back_body,
        in_specs=[pl.BlockSpec(memory_space=pltpu.SMEM)] + [vmem] * 8,
        out_specs=[pl.BlockSpec(memory_space=pltpu.HBM), vmem],
        out_shape=[
            jax.ShapeDtypeStruct((1, 2, ROWS, COLS), BF),
            jax.ShapeDtypeStruct((COLS, RANK2), F32),
        ],
        scratch_shapes=[
            pltpu.VMEM((2, ROWS, COLS), BF),
            pltpu.VMEM((RANK2, 2 * COLS), BF),
            pltpu.SemaphoreType.DMA((2, HALF // BACK)),
        ],
        compiler_params=pltpu.CompilerParams(vmem_limit_bytes=16 * MIB),
        cost_estimate=pl.CostEstimate(flops=4 * ROWS * 128 * 128, bytes_accessed=6 * MIB, transcendentals=0),
    )(half, f, c_own, c_other, inv, *us)


def swap_cores(x):
    return lax.ppermute(x, "c", [(0, 1), (1, 0)])


def pair(x, axis, size, flip):
    return lax.ppermute(x, axis, [(i, i ^ flip) for i in range(size)])


def plus(a, b):
    return (a.astype(F32) + b.astype(F32)).astype(BF)


def exchange(x, axes):
    return lax.all_to_all(x, axes, 0, 0)


def local(grads, momentum, error, q_warm):
    c = lax.axis_index("c").astype(jnp.int32)
    mine, theirs = c.reshape(1), (1 - c).reshape(1)

    with jax.named_scope("p_partial"):
        args = (grads, momentum, error, q_warm)
        mo_other, c_other, p_send = front(theirs, args, BF)
        p_got = swap_cores(p_send)
        mo_own, c_own, p_own = front(mine, args, F32)
        chip = (p_own + p_got.astype(F32)).astype(BF)
    with jax.named_scope("p_sum"):
        parts = exchange(chip.reshape(NX * NY, BLK, RANK2), ("x", "y"))
        part = sum_copies(parts, 1)[0]
        part = plus(part, pair(part, "z", NZ, 6))
        parts = jnp.stack([part] + [pair(part, "z", NZ, k) for k in (1, 2, 3)])
        p_mine = exchange(sum_copies(parts, NX * NY), ("x", "y")).reshape(HALF, RANK2)
        p_theirs = swap_cores(p_mine)
    with jax.named_scope("u_sum"):
        first = products(p_mine, c_own, None)
        u, gram = products(p_theirs, c_other, first)
        def tree(u, got):
            u, a, b, d = (t.astype(F32) for t in (u, *got))
            return ((u + a) + (b + d)).astype(BF)

        got = pair(u, "z", NZ, 6)
        got, inv, momentum_out = lax.optimization_barrier((got, *inverse(mine, gram, mo_own, mo_other)))
        u = plus(u, got)
        got = [pair(u, "z", NZ, k) for k in (1, 2, 3)]
        got, p_factor, f = lax.optimization_barrier((got, *factor(mine, inv, p_mine, p_theirs)))
        u = tree(u, got)
        got = [pair(u, "x", NX, k) for k in (1, 2, 3)]
    with jax.named_scope("back"):
        error_out, q_factor = back(mine, f, c_own, c_other, inv, (u, *got))
    return momentum_out, error_out, p_factor, q_factor


def solution(mesh):
    fine = Mesh(mesh.devices.reshape(NZ, NX, NY, NC), ("z", "x", "y", "c"))
    dp, tensor = ("z", "x"), ("y", "c")
    big = P(dp, None, None, tensor)
    return jax.shard_map(
        local,
        mesh=fine,
        in_specs=(big, big, big, P(tensor, None)),
        out_specs=(big, big, P(), P(tensor, None)),
        check_vma=False,
    )
```

```python
import jax
import jax.numpy as jnp
from jax import lax
from jax.experimental import pallas as pl
from jax.experimental.pallas import tpu as pltpu
from jax.sharding import Mesh
from jax.sharding import PartitionSpec as P

BF, F32 = jnp.bfloat16, jnp.float32
NZ, NX, NY, NC = 8, 4, 4, 2
ROWS, COLS, RANK2 = 4096, 128, 128
HALF = ROWS // NC
BLK = HALF // (NX * NY)
FRONT, PROD, BACK = 1024, 512, 256
PANEL = 8
MIB = 1 << 20


def dot(a, b, dims=((1,), (0,)), precision=None):
    return lax.dot_general(a, b, (dims, ((), ())), precision=precision, preferred_element_type=F32)


def left_lanes(shape):
    return lax.broadcasted_iota(jnp.int32, shape, len(shape) - 1) < RANK2 // 2


def front_body(half_ref, g_hbm, m_hbm, e_hbm, q_hbm, mo_ref, c_ref, p_ref, g_buf, m_buf, e_buf, q_buf, sem, q_sem):
    base = pl.multiple_of(half_ref[0] * HALF, HALF)

    def loads(k):
        here = pl.ds(pl.multiple_of(k * FRONT, FRONT), FRONT)
        there = pl.ds(pl.multiple_of(base + k * FRONT, FRONT), FRONT)
        return [
            pltpu.make_async_copy(hbm.at[0, :, there], buf.at[:, here], sem.at[i, k])
            for i, (hbm, buf) in enumerate(((m_hbm, m_buf), (g_hbm, g_buf), (e_hbm, e_buf)))
        ]

    load_q = pltpu.make_async_copy(q_hbm, q_buf, q_sem)
    load_q.start()
    for k in range(HALF // FRONT):
        for copy in loads(k):
            copy.start()
    load_q.wait()
    q = q_buf[...]
    left = left_lanes(q.shape)
    q_of = [jnp.where(left if group == 0 else ~left, q, jnp.zeros_like(q)) for group in range(2)]

    for k in range(HALF // FRONT):
        for copy in loads(k):
            copy.wait()
        rows = pl.ds(pl.multiple_of(k * FRONT, FRONT), FRONT)
        total = None
        for group in range(2):
            mo = (0.9 * m_buf[group, rows].astype(F32) + g_buf[group, rows].astype(F32)).astype(BF)
            co = (mo.astype(F32) + e_buf[group, rows].astype(F32)).astype(BF)
            mo_ref[group, rows] = mo
            c_ref[group, rows] = co
            term = dot(co, q_of[group])
            total = term if total is None else total + term
        p_ref[rows] = total.astype(p_ref.dtype)


def front(half, args, p_dtype):
    hbm, vmem = pl.BlockSpec(memory_space=pltpu.HBM), pl.BlockSpec(memory_space=pltpu.VMEM)
    return pl.pallas_call(
        front_body,
        in_specs=[pl.BlockSpec(memory_space=pltpu.SMEM)] + [hbm] * 4,
        out_specs=[vmem] * 3,
        out_shape=[pltpu.VMEM((2, HALF, COLS), BF), pltpu.VMEM((2, HALF, COLS), BF), pltpu.VMEM((HALF, RANK2), p_dtype)],
        scratch_shapes=[pltpu.VMEM((2, HALF, COLS), BF)] * 3
        + [pltpu.VMEM((COLS, RANK2), BF), pltpu.SemaphoreType.DMA((3, HALF // FRONT)), pltpu.SemaphoreType.DMA],
        compiler_params=pltpu.CompilerParams(vmem_limit_bytes=16 * MIB),
        cost_estimate=pl.CostEstimate(flops=2 * HALF * 256 * 128, bytes_accessed=4 * MIB, transcendentals=0),
    )(half, *(pltpu.with_memory_space_constraint(x, pltpu.HBM) for x in args))


def sum_copies_body(x_ref, o_ref):
    terms = [x_ref[k].astype(F32) for k in range(x_ref.shape[0])]
    while len(terms) > 1:
        terms = [a + b for a, b in zip(terms[::2], terms[1::2])]
    total = terms[0].astype(BF)
    for k in range(o_ref.shape[0]):
        o_ref[k] = total


def sum_copies(x, copies):
    return pl.pallas_call(
        sum_copies_body,
        out_shape=jax.ShapeDtypeStruct((copies, *x.shape[1:]), BF),
        compiler_params=pltpu.CompilerParams(vmem_limit_bytes=16 * MIB),
    )(x)


def products_body(p_ref, c_ref, *rest):
    u_ref, g_ref = rest[-2:]
    n = RANK2 // 2
    u0 = u1 = gram = None
    for k in range(HALF // PROD):
        rows = pl.ds(k * PROD, PROD)
        p = p_ref[rows]
        pt = p.T
        a, b, c = dot(pt[:n], c_ref[0, rows]), dot(pt[n:], c_ref[1, rows]), dot(pt, p)
        u0, u1, gram = (a, b, c) if u0 is None else (u0 + a, u1 + b, gram + c)
    u = jnp.concatenate([u0, u1], axis=0)
    if len(rest) == 2:
        u_ref[...] = u
        g_ref[...] = gram
    else:
        u_ref[...] = (u + rest[0][...]).astype(BF)
        g_ref[...] = gram + rest[1][...]


def products(p, c, before):
    last = before is not None
    return pl.pallas_call(
        products_body,
        out_shape=[
            jax.ShapeDtypeStruct((RANK2, COLS), BF if last else F32),
            jax.ShapeDtypeStruct((RANK2, RANK2), F32),
        ],
        compiler_params=pltpu.CompilerParams(vmem_limit_bytes=16 * MIB),
        cost_estimate=pl.CostEstimate(flops=2 * HALF * 256 * 128, bytes_accessed=2 * MIB, transcendentals=0),
    )(p, c, *(before if last else ()))


def invert(g_ref, o_ref):
    n, t = RANK2 // 2, PANEL
    tiles = n // t
    lane = lax.broadcasted_iota(jnp.int32, (t, 2 * n), 1)
    sub = lax.broadcasted_iota(jnp.int32, (t, 2 * n), 0)
    left = lane < n

    def spread(x):
        return jnp.broadcast_to(x, (t, 2 * n))

    both = []
    for s in range(2):
        for i in range(tiles):
            x = g_ref[s * n + t * i : s * n + t * i + t]
            x = pltpu.roll(x, n, 1) if s else x
            both.append(jnp.where(left, x, jnp.where(lane == sub + (t * i + n), 1.0, 0.0)))

    for top in range(tiles):
        first, live, out = top * t, tiles - top, []
        for s in range(2):
            a = list(both[s * live : (s + 1) * live])
            forward = full = a[0]
            c = [spread(full[:, first + j : first + j + 1]) for j in range(t)]
            pivots = None
            for j in range(t):
                d = spread(c[j][j : j + 1])
                pivots = d if j == 0 else jnp.where(sub == j, d, pivots)
                scale = 1.0 / d
                factor = c[j] * scale
                row = spread(forward[j : j + 1])
                full = jnp.where(sub == j, row * scale, full - factor * row)
                forward = forward - jnp.where(sub > j, factor, 0.0) * row
                for q in range(j + 1, t):
                    value = spread(c[j][q : q + 1])
                    c[q] = jnp.where(sub == j, value * scale, c[q] - factor * value)
            y = forward * lax.rsqrt(pivots)
            o_ref[pl.ds(s * n + first, t)] = jnp.where(left, 0.0, y) if s else jnp.where(left, pltpu.roll(y, n, 1), 0.0)
            solved = [spread(full[j : j + 1]) for j in range(t)]
            for x in a[1:]:
                columns = [spread(x[:, first + j : first + j + 1]) for j in range(t)]
                for j in range(t):
                    x = x - columns[j] * solved[j]
                out.append(x)
        both = out


def inverse(gram):
    return pl.pallas_call(
        invert,
        out_shape=jax.ShapeDtypeStruct((RANK2, RANK2), F32),
        compiler_params=pltpu.CompilerParams(vmem_limit_bytes=16 * MIB),
        cost_estimate=pl.CostEstimate(flops=64**3, bytes_accessed=6 * MIB, transcendentals=128),
    )(gram)


def store_body(half_ref, own_ref, other_ref, m_hbm, sem):
    copies = []
    for i, ref in enumerate((own_ref, other_ref)):
        half = half_ref[0] if i == 0 else 1 - half_ref[0]
        there = pl.ds(pl.multiple_of(half * HALF, HALF), HALF)
        copies.append(pltpu.make_async_copy(ref, m_hbm.at[0, :, there], sem.at[i]))
        copies[-1].start()
    for copy in copies:
        copy.wait()


def store(half, own, other):
    vmem = pl.BlockSpec(memory_space=pltpu.VMEM)
    return pl.pallas_call(
        store_body,
        in_specs=[pl.BlockSpec(memory_space=pltpu.SMEM), vmem, vmem],
        out_specs=pl.BlockSpec(memory_space=pltpu.HBM),
        out_shape=jax.ShapeDtypeStruct((1, 2, ROWS, COLS), BF),
        scratch_shapes=[pltpu.SemaphoreType.DMA((2,))],
        compiler_params=pltpu.CompilerParams(vmem_limit_bytes=16 * MIB),
        cost_estimate=pl.CostEstimate(flops=0, bytes_accessed=4 * MIB, transcendentals=0),
    )(half, own, other)


def factor_body(half_ref, l_ref, po_ref, pt_ref, p_hbm, f_ref, w_ref, sem):
    inv_t = l_ref[...].T
    hi = inv_t.astype(BF)
    w_ref[:RANK2] = hi
    w_ref[RANK2:] = (inv_t - hi.astype(F32)).astype(BF)
    weights = w_ref[...]
    moves = []
    for which, p_ref in enumerate((po_ref, pt_ref)):
        half = half_ref[0] if which == 0 else 1 - half_ref[0]
        for k in range(HALF // BACK):
            p = p_ref[pl.ds(k * BACK, BACK)]
            f_ref[pl.ds(which * HALF + k * BACK, BACK)] = dot(jnp.concatenate([p, p], axis=1), weights).astype(BF)
        there = pl.ds(pl.multiple_of(half * HALF, HALF), HALF)
        moves.append(pltpu.make_async_copy(f_ref.at[pl.ds(which * HALF, HALF)], p_hbm.at[there], sem.at[which]))
        moves[-1].start()
    for copy in moves:
        copy.wait()


def factor(half, inv, p_own, p_other):
    hbm, vmem = pl.BlockSpec(memory_space=pltpu.HBM), pl.BlockSpec(memory_space=pltpu.VMEM)
    return pl.pallas_call(
        factor_body,
        in_specs=[pl.BlockSpec(memory_space=pltpu.SMEM)] + [vmem] * 3,
        out_specs=[hbm, vmem],
        out_shape=[jax.ShapeDtypeStruct((ROWS, RANK2), BF), pltpu.VMEM((ROWS, RANK2), BF)],
        scratch_shapes=[pltpu.VMEM((2 * RANK2, RANK2), BF), pltpu.SemaphoreType.DMA((2,))],
        compiler_params=pltpu.CompilerParams(vmem_limit_bytes=16 * MIB),
        cost_estimate=pl.CostEstimate(flops=4 * ROWS * 128 * 128, bytes_accessed=6 * MIB, transcendentals=0),
    )(half, inv, p_own, p_other)


def split(x):
    hi = x.astype(BF)
    return hi, (x - hi.astype(F32)).astype(BF)


def back_body(half_ref, f_ref, co_ref, ct_ref, l_ref, u_ref, a_ref, b_ref, d_ref, e_hbm, q_ref, e_buf, w_ref, sem):
    u, a, b, d = (t[...].astype(F32) for t in (u_ref, a_ref, b_ref, d_ref))
    (ih, il), (uh, ul) = split(l_ref[...]), split(((u + a) + (b + d)) * (1.0 / (NZ * NX)))
    qt = dot(jnp.concatenate([ih, il], axis=1), jnp.concatenate([uh, uh], axis=0)) + dot(ih, ul)
    q_ref[...] = qt
    qt = qt.astype(BF)
    top = lax.broadcasted_iota(jnp.int32, qt.shape, 0) < RANK2 // 2
    zero = jnp.zeros_like(qt)
    w_ref[...] = jnp.concatenate([jnp.where(top, qt, zero), jnp.where(top, zero, qt)], axis=1)
    weights = w_ref[...]
    copies = []
    for which, c_ref in enumerate((co_ref, ct_ref)):
        half = half_ref[0] if which == 0 else 1 - half_ref[0]
        for k in range(HALF // BACK):
            here = pl.ds(which * HALF + k * BACK, BACK)
            there = pl.ds(pl.multiple_of(half * HALF + k * BACK, BACK), BACK)
            approx = dot(f_ref[here], weights)
            for group in range(2):
                c = c_ref[group, pl.ds(k * BACK, BACK)].astype(F32)
                e_buf[group, here] = (c - approx[:, group * COLS : (group + 1) * COLS]).astype(BF)
            copies.append(pltpu.make_async_copy(e_buf.at[:, here], e_hbm.at[0, :, there], sem.at[which, k]))
            copies[-1].start()
    q_ref[...] = q_ref[...].T
    for copy in copies:
        copy.wait()


def back(half, f, c_own, c_other, inv, us):
    vmem = pl.BlockSpec(memory_space=pltpu.VMEM)
    return pl.pallas_call(
        back_body,
        in_specs=[pl.BlockSpec(memory_space=pltpu.SMEM)] + [vmem] * 8,
        out_specs=[pl.BlockSpec(memory_space=pltpu.HBM), vmem],
        out_shape=[
            jax.ShapeDtypeStruct((1, 2, ROWS, COLS), BF),
            jax.ShapeDtypeStruct((COLS, RANK2), F32),
        ],
        scratch_shapes=[
            pltpu.VMEM((2, ROWS, COLS), BF),
            pltpu.VMEM((RANK2, 2 * COLS), BF),
            pltpu.SemaphoreType.DMA((2, HALF // BACK)),
        ],
        compiler_params=pltpu.CompilerParams(vmem_limit_bytes=16 * MIB),
        cost_estimate=pl.CostEstimate(flops=4 * ROWS * 128 * 128, bytes_accessed=6 * MIB, transcendentals=0),
    )(half, f, c_own, c_other, inv, *us)


def swap_cores(x):
    return lax.ppermute(x, "c", [(0, 1), (1, 0)])


def pair(x, axis, size, flip):
    return lax.ppermute(x, axis, [(i, i ^ flip) for i in range(size)])


def plus(a, b):
    return (a.astype(F32) + b.astype(F32)).astype(BF)


def exchange(x, axes):
    return lax.all_to_all(x, axes, 0, 0)


def local(grads, momentum, error, q_warm):
    c = lax.axis_index("c").astype(jnp.int32)
    mine, theirs = c.reshape(1), (1 - c).reshape(1)

    with jax.named_scope("p_partial"):
        args = (grads, momentum, error, q_warm)
        mo_other, c_other, p_send = front(theirs, args, BF)
        p_got = swap_cores(p_send)
        mo_own, c_own, p_own = front(mine, args, F32)
        chip = (p_own + p_got.astype(F32)).astype(BF)
    with jax.named_scope("p_sum"):
        parts = exchange(chip.reshape(NX * NY, BLK, RANK2), ("x", "y"))
        part = sum_copies(parts, 1)[0]
        part = plus(part, pair(part, "z", NZ, 6))
        got = [pair(part, "z", NZ, k) for k in (1, 2, 3)]
        got, momentum_out = lax.optimization_barrier((got, store(mine, mo_own, mo_other)))
        parts = jnp.stack([part] + got)
        p_mine = exchange(sum_copies(parts, NX * NY), ("x", "y")).reshape(HALF, RANK2)
        p_theirs = swap_cores(p_mine)
    with jax.named_scope("u_sum"):
        first = products(p_mine, c_own, None)
        u, gram = products(p_theirs, c_other, first)
        def tree(u, got):
            u, a, b, d = (t.astype(F32) for t in (u, *got))
            return ((u + a) + (b + d)).astype(BF)

        got = pair(u, "z", NZ, 6)
        got, inv = lax.optimization_barrier((got, inverse(gram)))
        u = plus(u, got)
        got = [pair(u, "z", NZ, k) for k in (1, 2, 3)]
        got, p_factor, f = lax.optimization_barrier((got, *factor(mine, inv, p_mine, p_theirs)))
        u = tree(u, got)
        got = [pair(u, "x", NX, k) for k in (1, 2, 3)]
    with jax.named_scope("back"):
        error_out, q_factor = back(mine, f, c_own, c_other, inv, (u, *got))
    return momentum_out, error_out, p_factor, q_factor


def solution(mesh):
    fine = Mesh(mesh.devices.reshape(NZ, NX, NY, NC), ("z", "x", "y", "c"))
    dp, tensor = ("z", "x"), ("y", "c")
    big = P(dp, None, None, tensor)
    return jax.shard_map(
        local,
        mesh=fine,
        in_specs=(big, big, big, P(tensor, None)),
        out_specs=(big, big, P(), P(tensor, None)),
        check_vma=False,
    )
```

```python
import jax
import jax.numpy as jnp
from jax import lax
from jax.experimental import pallas as pl
from jax.experimental.pallas import tpu as pltpu
from jax.sharding import Mesh
from jax.sharding import PartitionSpec as P

BF, F32 = jnp.bfloat16, jnp.float32
NZ, NX, NY, NC = 8, 4, 4, 2
ROWS, COLS, RANK2 = 4096, 128, 128
HALF = ROWS // NC
BLK = HALF // (NX * NY)
FRONT, PROD, BACK = 1024, 512, 256
PANEL = 8
MIB = 1 << 20


def dot(a, b, dims=((1,), (0,)), precision=None):
    return lax.dot_general(a, b, (dims, ((), ())), precision=precision, preferred_element_type=F32)


def left_lanes(shape):
    return lax.broadcasted_iota(jnp.int32, shape, len(shape) - 1) < RANK2 // 2


def front_body(half_ref, g_hbm, m_hbm, e_hbm, q_hbm, *rest):
    first = len(rest) == 13
    ahead, rest = (rest[3:6], rest[:3] + rest[6:]) if first else (rest[:3], rest[3:])
    mo_ref, c_ref, p_ref, g_buf, m_buf, e_buf, q_buf, sem, q_sem, *more = rest
    base = pl.multiple_of(half_ref[0] * HALF, HALF)
    hbm, buf = (m_hbm, g_hbm, e_hbm), (m_buf, g_buf, e_buf)

    def loads(k):
        here = pl.ds(k * FRONT, FRONT)
        there = pl.ds(pl.multiple_of(base + k * FRONT, FRONT), FRONT)
        return [pltpu.make_async_copy(hbm[i].at[0, :, there], buf[i].at[:, here], sem.at[i, k]) for i in range(3)]

    load_q = pltpu.make_async_copy(q_hbm, q_buf, q_sem)
    load_q.start()
    chunks = range(HALF // FRONT)
    mine = chunks if first else chunks[1:]
    for k in mine:
        for copy in loads(k):
            copy.start()
    extra = []
    if first:
        there = pl.ds(pl.multiple_of(HALF - base, HALF), FRONT)
        extra = [pltpu.make_async_copy(hbm[i].at[0, :, there], ahead[i], more[0].at[i]) for i in range(3)]
    for copy in extra:
        copy.start()
    load_q.wait()
    q = q_buf[...]
    left = left_lanes(q.shape)
    q_of = [jnp.where(left if group == 0 else ~left, q, jnp.zeros_like(q)) for group in range(2)]
    for k in chunks:
        rows = pl.ds(k * FRONT, FRONT)
        if k in mine:
            for copy in loads(k):
                copy.wait()
        total = None
        for group in range(2):
            m, g, e = (x[group, rows].astype(F32) for x in (buf if k in mine else ahead))
            mo = (0.9 * m + g).astype(BF)
            co = (mo.astype(F32) + e).astype(BF)
            mo_ref[group, rows] = mo
            c_ref[group, rows] = co
            term = dot(co, q_of[group])
            total = term if total is None else total + term
        p_ref[rows] = total.astype(p_ref.dtype)
    for copy in extra:
        copy.wait()


def front(half, args, ahead):
    hbm, vmem = pl.BlockSpec(memory_space=pltpu.HBM), pl.BlockSpec(memory_space=pltpu.VMEM)
    first = ahead is None
    part = pltpu.VMEM((2, HALF, COLS), BF)
    return pl.pallas_call(
        front_body,
        in_specs=[pl.BlockSpec(memory_space=pltpu.SMEM)] + [hbm] * 4 + [vmem] * (0 if first else 3),
        out_specs=[vmem] * (6 if first else 3),
        out_shape=[part, part, pltpu.VMEM((HALF, RANK2), BF if first else F32)]
        + [pltpu.VMEM((2, FRONT, COLS), BF)] * (3 if first else 0),
        scratch_shapes=[pltpu.VMEM((2, HALF, COLS), BF)] * 3
        + [pltpu.VMEM((COLS, RANK2), BF), pltpu.SemaphoreType.DMA((3, HALF // FRONT)), pltpu.SemaphoreType.DMA]
        + [pltpu.SemaphoreType.DMA((3,))] * first,
        compiler_params=pltpu.CompilerParams(vmem_limit_bytes=16 * MIB),
        cost_estimate=pl.CostEstimate(flops=2 * HALF * 256 * 128, bytes_accessed=4 * MIB, transcendentals=0),
    )(half, *(pltpu.with_memory_space_constraint(x, pltpu.HBM) for x in args), *(ahead or ()))


def sum_copies_body(x_ref, o_ref):
    terms = [x_ref[k].astype(F32) for k in range(x_ref.shape[0])]
    while len(terms) > 1:
        terms = [a + b for a, b in zip(terms[::2], terms[1::2])]
    total = terms[0].astype(BF)
    for k in range(o_ref.shape[0]):
        o_ref[k] = total


def sum_copies(x, copies):
    return pl.pallas_call(
        sum_copies_body,
        out_shape=jax.ShapeDtypeStruct((copies, *x.shape[1:]), BF),
        compiler_params=pltpu.CompilerParams(vmem_limit_bytes=16 * MIB),
    )(x)


def products_body(p_ref, c_ref, *rest):
    u_ref, g_ref = rest[-2:]
    n = RANK2 // 2
    u0 = u1 = gram = None
    for k in range(HALF // PROD):
        rows = pl.ds(k * PROD, PROD)
        p = p_ref[rows]
        pt = p.T
        a, b, c = dot(pt[:n], c_ref[0, rows]), dot(pt[n:], c_ref[1, rows]), dot(pt, p)
        u0, u1, gram = (a, b, c) if u0 is None else (u0 + a, u1 + b, gram + c)
    u = jnp.concatenate([u0, u1], axis=0)
    if len(rest) == 2:
        u_ref[...] = u
        g_ref[...] = gram
    else:
        u_ref[...] = (u + rest[0][...]).astype(BF)
        g_ref[...] = gram + rest[1][...]


def products(p, c, before):
    last = before is not None
    return pl.pallas_call(
        products_body,
        out_shape=[
            jax.ShapeDtypeStruct((RANK2, COLS), BF if last else F32),
            jax.ShapeDtypeStruct((RANK2, RANK2), F32),
        ],
        compiler_params=pltpu.CompilerParams(vmem_limit_bytes=16 * MIB),
        cost_estimate=pl.CostEstimate(flops=2 * HALF * 256 * 128, bytes_accessed=2 * MIB, transcendentals=0),
    )(p, c, *(before if last else ()))


def invert(g_ref, o_ref):
    n, t = RANK2 // 2, PANEL
    tiles = n // t
    lane = lax.broadcasted_iota(jnp.int32, (t, 2 * n), 1)
    sub = lax.broadcasted_iota(jnp.int32, (t, 2 * n), 0)
    left = lane < n

    def spread(x):
        return jnp.broadcast_to(x, (t, 2 * n))

    both = []
    for s in range(2):
        for i in range(tiles):
            x = g_ref[s * n + t * i : s * n + t * i + t]
            x = pltpu.roll(x, n, 1) if s else x
            both.append(jnp.where(left, x, jnp.where(lane == sub + (t * i + n), 1.0, 0.0)))

    for top in range(tiles):
        first, live, out = top * t, tiles - top, []
        for s in range(2):
            a = list(both[s * live : (s + 1) * live])
            forward = full = a[0]
            c = [spread(full[:, first + j : first + j + 1]) for j in range(t)]
            pivots = None
            for j in range(t):
                d = spread(c[j][j : j + 1])
                pivots = d if j == 0 else jnp.where(sub == j, d, pivots)
                scale = 1.0 / d
                factor = c[j] * scale
                row = spread(forward[j : j + 1])
                full = jnp.where(sub == j, row * scale, full - factor * row)
                forward = forward - jnp.where(sub > j, factor, 0.0) * row
                for q in range(j + 1, t):
                    value = spread(c[j][q : q + 1])
                    c[q] = jnp.where(sub == j, value * scale, c[q] - factor * value)
            y = forward * lax.rsqrt(pivots)
            o_ref[pl.ds(s * n + first, t)] = jnp.where(left, 0.0, y) if s else jnp.where(left, pltpu.roll(y, n, 1), 0.0)
            solved = [spread(full[j : j + 1]) for j in range(t)]
            for x in a[1:]:
                columns = [spread(x[:, first + j : first + j + 1]) for j in range(t)]
                for j in range(t):
                    x = x - columns[j] * solved[j]
                out.append(x)
        both = out


def inverse(gram):
    return pl.pallas_call(
        invert,
        out_shape=jax.ShapeDtypeStruct((RANK2, RANK2), F32),
        compiler_params=pltpu.CompilerParams(vmem_limit_bytes=16 * MIB),
        cost_estimate=pl.CostEstimate(flops=64**3, bytes_accessed=6 * MIB, transcendentals=128),
    )(gram)


def store_body(half_ref, own_ref, other_ref, m_hbm, sem):
    copies = []
    for i, ref in enumerate((own_ref, other_ref)):
        half = half_ref[0] if i == 0 else 1 - half_ref[0]
        there = pl.ds(pl.multiple_of(half * HALF, HALF), HALF)
        copies.append(pltpu.make_async_copy(ref, m_hbm.at[0, :, there], sem.at[i]))
        copies[-1].start()
    for copy in copies:
        copy.wait()


def store(half, own, other):
    vmem = pl.BlockSpec(memory_space=pltpu.VMEM)
    return pl.pallas_call(
        store_body,
        in_specs=[pl.BlockSpec(memory_space=pltpu.SMEM), vmem, vmem],
        out_specs=pl.BlockSpec(memory_space=pltpu.HBM),
        out_shape=jax.ShapeDtypeStruct((1, 2, ROWS, COLS), BF),
        scratch_shapes=[pltpu.SemaphoreType.DMA((2,))],
        compiler_params=pltpu.CompilerParams(vmem_limit_bytes=16 * MIB),
        cost_estimate=pl.CostEstimate(flops=0, bytes_accessed=4 * MIB, transcendentals=0),
    )(half, own, other)


def factor_body(half_ref, l_ref, po_ref, pt_ref, p_hbm, f_ref, w_ref, sem):
    inv_t = l_ref[...].T
    hi = inv_t.astype(BF)
    w_ref[:RANK2] = hi
    w_ref[RANK2:] = (inv_t - hi.astype(F32)).astype(BF)
    weights = w_ref[...]
    moves = []
    for which, p_ref in enumerate((po_ref, pt_ref)):
        half = half_ref[0] if which == 0 else 1 - half_ref[0]
        for k in range(HALF // BACK):
            p = p_ref[pl.ds(k * BACK, BACK)]
            f_ref[pl.ds(which * HALF + k * BACK, BACK)] = dot(jnp.concatenate([p, p], axis=1), weights).astype(BF)
        there = pl.ds(pl.multiple_of(half * HALF, HALF), HALF)
        moves.append(pltpu.make_async_copy(f_ref.at[pl.ds(which * HALF, HALF)], p_hbm.at[there], sem.at[which]))
        moves[-1].start()
    for copy in moves:
        copy.wait()


def factor(half, inv, p_own, p_other):
    hbm, vmem = pl.BlockSpec(memory_space=pltpu.HBM), pl.BlockSpec(memory_space=pltpu.VMEM)
    return pl.pallas_call(
        factor_body,
        in_specs=[pl.BlockSpec(memory_space=pltpu.SMEM)] + [vmem] * 3,
        out_specs=[hbm, vmem],
        out_shape=[jax.ShapeDtypeStruct((ROWS, RANK2), BF), pltpu.VMEM((ROWS, RANK2), BF)],
        scratch_shapes=[pltpu.VMEM((2 * RANK2, RANK2), BF), pltpu.SemaphoreType.DMA((2,))],
        compiler_params=pltpu.CompilerParams(vmem_limit_bytes=16 * MIB),
        cost_estimate=pl.CostEstimate(flops=4 * ROWS * 128 * 128, bytes_accessed=6 * MIB, transcendentals=0),
    )(half, inv, p_own, p_other)


def split(x):
    hi = x.astype(BF)
    return hi, (x - hi.astype(F32)).astype(BF)


def back_body(half_ref, f_ref, co_ref, ct_ref, l_ref, u_ref, a_ref, b_ref, d_ref, e_hbm, q_ref, e_buf, w_ref, sem):
    u, a, b, d = (t[...].astype(F32) for t in (u_ref, a_ref, b_ref, d_ref))
    (ih, il), (uh, ul) = split(l_ref[...]), split(((u + a) + (b + d)) * (1.0 / (NZ * NX)))
    qt = dot(jnp.concatenate([ih, il], axis=1), jnp.concatenate([uh, uh], axis=0)) + dot(ih, ul)
    q_ref[...] = qt
    qt = qt.astype(BF)
    top = lax.broadcasted_iota(jnp.int32, qt.shape, 0) < RANK2 // 2
    zero = jnp.zeros_like(qt)
    w_ref[...] = jnp.concatenate([jnp.where(top, qt, zero), jnp.where(top, zero, qt)], axis=1)
    weights = w_ref[...]
    copies = []
    for which, c_ref in enumerate((co_ref, ct_ref)):
        half = half_ref[0] if which == 0 else 1 - half_ref[0]
        for k in range(HALF // BACK):
            here = pl.ds(which * HALF + k * BACK, BACK)
            there = pl.ds(pl.multiple_of(half * HALF + k * BACK, BACK), BACK)
            approx = dot(f_ref[here], weights)
            for group in range(2):
                c = c_ref[group, pl.ds(k * BACK, BACK)].astype(F32)
                e_buf[group, here] = (c - approx[:, group * COLS : (group + 1) * COLS]).astype(BF)
            copies.append(pltpu.make_async_copy(e_buf.at[:, here], e_hbm.at[0, :, there], sem.at[which, k]))
            copies[-1].start()
    q_ref[...] = q_ref[...].T
    for copy in copies:
        copy.wait()


def back(half, f, c_own, c_other, inv, us):
    vmem = pl.BlockSpec(memory_space=pltpu.VMEM)
    return pl.pallas_call(
        back_body,
        in_specs=[pl.BlockSpec(memory_space=pltpu.SMEM)] + [vmem] * 8,
        out_specs=[pl.BlockSpec(memory_space=pltpu.HBM), vmem],
        out_shape=[
            jax.ShapeDtypeStruct((1, 2, ROWS, COLS), BF),
            jax.ShapeDtypeStruct((COLS, RANK2), F32),
        ],
        scratch_shapes=[
            pltpu.VMEM((2, ROWS, COLS), BF),
            pltpu.VMEM((RANK2, 2 * COLS), BF),
            pltpu.SemaphoreType.DMA((2, HALF // BACK)),
        ],
        compiler_params=pltpu.CompilerParams(vmem_limit_bytes=16 * MIB),
        cost_estimate=pl.CostEstimate(flops=4 * ROWS * 128 * 128, bytes_accessed=6 * MIB, transcendentals=0),
    )(half, f, c_own, c_other, inv, *us)


def swap_cores(x):
    return lax.ppermute(x, "c", [(0, 1), (1, 0)])


def pair(x, axis, size, flip):
    return lax.ppermute(x, axis, [(i, i ^ flip) for i in range(size)])


def plus(a, b):
    return (a.astype(F32) + b.astype(F32)).astype(BF)


def exchange(x, axes):
    return lax.all_to_all(x, axes, 0, 0)


def local(grads, momentum, error, q_warm):
    c = lax.axis_index("c").astype(jnp.int32)
    mine, theirs = c.reshape(1), (1 - c).reshape(1)

    with jax.named_scope("p_partial"):
        args = (grads, momentum, error, q_warm)
        mo_other, c_other, p_send, *ahead = front(theirs, args, None)
        p_got = swap_cores(p_send)
        mo_own, c_own, p_own = front(mine, args, ahead)
        chip = (p_own + p_got.astype(F32)).astype(BF)
    with jax.named_scope("p_sum"):
        parts = exchange(chip.reshape(NX * NY, BLK, RANK2), ("y", "x"))
        part = sum_copies(parts, 1)[0]
        part = plus(part, pair(part, "z", NZ, 6))
        got = [pair(part, "z", NZ, k) for k in (1, 2, 3)]
        got, momentum_out = lax.optimization_barrier((got, store(mine, mo_own, mo_other)))
        parts = jnp.stack([part] + got)
        p_mine = exchange(sum_copies(parts, NX * NY), ("y", "x")).reshape(HALF, RANK2)
        p_theirs = swap_cores(p_mine)
    with jax.named_scope("u_sum"):
        first = products(p_mine, c_own, None)
        u, gram = products(p_theirs, c_other, first)
        def tree(u, got):
            u, a, b, d = (t.astype(F32) for t in (u, *got))
            return ((u + a) + (b + d)).astype(BF)

        got = pair(u, "z", NZ, 6)
        got, inv = lax.optimization_barrier((got, inverse(gram)))
        u = plus(u, got)
        got = [pair(u, "z", NZ, k) for k in (1, 2, 3)]
        got, p_factor, f = lax.optimization_barrier((got, *factor(mine, inv, p_mine, p_theirs)))
        u = tree(u, got)
        got = [pair(u, "x", NX, k) for k in (1, 2, 3)]
    with jax.named_scope("back"):
        error_out, q_factor = back(mine, f, c_own, c_other, inv, (u, *got))
    return momentum_out, error_out, p_factor, q_factor


def solution(mesh):
    fine = Mesh(mesh.devices.reshape(NZ, NX, NY, NC), ("z", "x", "y", "c"))
    dp, tensor = ("z", "x"), ("y", "c")
    big = P(dp, None, None, tensor)
    return jax.shard_map(
        local,
        mesh=fine,
        in_specs=(big, big, big, P(tensor, None)),
        out_specs=(big, big, P(), P(tensor, None)),
        check_vma=False,
    )
```

```python
import jax
import jax.numpy as jnp
from jax import lax
from jax.experimental import pallas as pl
from jax.experimental.pallas import tpu as pltpu
from jax.sharding import Mesh
from jax.sharding import PartitionSpec as P

BF, F32 = jnp.bfloat16, jnp.float32
NZ, NX, NY, NC = 8, 4, 4, 2
ROWS, COLS, RANK2 = 4096, 128, 128
HALF = ROWS // NC
BLK = HALF // (NX * NY)
FRONT, PROD, BACK = 1024, 512, 256
PANEL = 8
MIB = 1 << 20


def dot(a, b, dims=((1,), (0,)), precision=None):
    return lax.dot_general(a, b, (dims, ((), ())), precision=precision, preferred_element_type=F32)


def left_lanes(shape):
    return lax.broadcasted_iota(jnp.int32, shape, len(shape) - 1) < RANK2 // 2


def front_body(half_ref, g_hbm, m_hbm, e_hbm, q_hbm, *rest):
    first = len(rest) == 13
    ahead, rest = (rest[3:6], rest[:3] + rest[6:]) if first else (rest[:3], rest[3:])
    mo_ref, c_ref, p_ref, g_buf, m_buf, e_buf, q_buf, sem, q_sem, *more = rest
    base = pl.multiple_of(half_ref[0] * HALF, HALF)
    hbm, buf = (m_hbm, g_hbm, e_hbm), (m_buf, g_buf, e_buf)

    def loads(k):
        here = pl.ds(k * FRONT, FRONT)
        there = pl.ds(pl.multiple_of(base + k * FRONT, FRONT), FRONT)
        return [pltpu.make_async_copy(hbm[i].at[0, :, there], buf[i].at[:, here], sem.at[i, k]) for i in range(3)]

    load_q = pltpu.make_async_copy(q_hbm, q_buf, q_sem)
    load_q.start()
    chunks = range(HALF // FRONT)
    mine = chunks if first else chunks[1:]
    for k in mine:
        for copy in loads(k):
            copy.start()
    extra = []
    if first:
        there = pl.ds(pl.multiple_of(HALF - base, HALF), FRONT)
        extra = [pltpu.make_async_copy(hbm[i].at[0, :, there], ahead[i], more[0].at[i]) for i in range(3)]
    for copy in extra:
        copy.start()
    load_q.wait()
    q = q_buf[...]
    left = left_lanes(q.shape)
    q_of = [jnp.where(left if group == 0 else ~left, q, jnp.zeros_like(q)) for group in range(2)]
    for k in chunks:
        rows = pl.ds(k * FRONT, FRONT)
        if k in mine:
            for copy in loads(k):
                copy.wait()
        total = None
        for group in range(2):
            m, g, e = (x[group, rows].astype(F32) for x in (buf if k in mine else ahead))
            mo = (0.9 * m + g).astype(BF)
            co = (mo.astype(F32) + e).astype(BF)
            mo_ref[group, rows] = mo
            c_ref[group, rows] = co
            term = dot(co, q_of[group])
            total = term if total is None else total + term
        p_ref[rows] = total.astype(p_ref.dtype)
    for copy in extra:
        copy.wait()


def front(half, args, ahead):
    hbm, vmem = pl.BlockSpec(memory_space=pltpu.HBM), pl.BlockSpec(memory_space=pltpu.VMEM)
    first = ahead is None
    part = pltpu.VMEM((2, HALF, COLS), BF)
    return pl.pallas_call(
        front_body,
        in_specs=[pl.BlockSpec(memory_space=pltpu.SMEM)] + [hbm] * 4 + [vmem] * (0 if first else 3),
        out_specs=[vmem] * (6 if first else 3),
        out_shape=[part, part, pltpu.VMEM((HALF, RANK2), BF if first else F32)]
        + [pltpu.VMEM((2, FRONT, COLS), BF)] * (3 if first else 0),
        scratch_shapes=[pltpu.VMEM((2, HALF, COLS), BF)] * 3
        + [pltpu.VMEM((COLS, RANK2), BF), pltpu.SemaphoreType.DMA((3, HALF // FRONT)), pltpu.SemaphoreType.DMA]
        + [pltpu.SemaphoreType.DMA((3,))] * first,
        compiler_params=pltpu.CompilerParams(vmem_limit_bytes=16 * MIB),
        cost_estimate=pl.CostEstimate(flops=2 * HALF * 256 * 128, bytes_accessed=4 * MIB, transcendentals=0),
    )(half, *(pltpu.with_memory_space_constraint(x, pltpu.HBM) for x in args), *(ahead or ()))


def sum_copies_body(x_ref, o_ref):
    terms = [x_ref[k].astype(F32) for k in range(x_ref.shape[0])]
    while len(terms) > 1:
        terms = [a + b for a, b in zip(terms[::2], terms[1::2])]
    total = terms[0].astype(BF)
    for k in range(o_ref.shape[0]):
        o_ref[k] = total


def sum_copies(x, copies):
    return pl.pallas_call(
        sum_copies_body,
        out_shape=jax.ShapeDtypeStruct((copies, *x.shape[1:]), BF),
        compiler_params=pltpu.CompilerParams(vmem_limit_bytes=16 * MIB),
    )(x)


def products_body(p_ref, c_ref, *rest):
    u_ref, g_ref = rest[-2:]
    n = RANK2 // 2
    u0 = u1 = gram = None
    for k in range(HALF // PROD):
        rows = pl.ds(k * PROD, PROD)
        p = p_ref[rows]
        pt = p.T
        a, b, c = dot(pt[:n], c_ref[0, rows]), dot(pt[n:], c_ref[1, rows]), dot(pt, p)
        u0, u1, gram = (a, b, c) if u0 is None else (u0 + a, u1 + b, gram + c)
    u = jnp.concatenate([u0, u1], axis=0)
    if len(rest) == 2:
        u_ref[...] = u
        g_ref[...] = gram
    else:
        u_ref[...] = (u + rest[0][...]).astype(BF)
        g_ref[...] = gram + rest[1][...]


def products(p, c, before):
    last = before is not None
    return pl.pallas_call(
        products_body,
        out_shape=[
            jax.ShapeDtypeStruct((RANK2, COLS), BF if last else F32),
            jax.ShapeDtypeStruct((RANK2, RANK2), F32),
        ],
        compiler_params=pltpu.CompilerParams(vmem_limit_bytes=16 * MIB),
        cost_estimate=pl.CostEstimate(flops=2 * HALF * 256 * 128, bytes_accessed=2 * MIB, transcendentals=0),
    )(p, c, *(before if last else ()))


def invert(g_ref, o_ref):
    n, t = RANK2 // 2, PANEL
    tiles = n // t
    lane = lax.broadcasted_iota(jnp.int32, (t, 2 * n), 1)
    sub = lax.broadcasted_iota(jnp.int32, (t, 2 * n), 0)
    left = lane < n

    def spread(x):
        return jnp.broadcast_to(x, (t, 2 * n))

    both = []
    for s in range(2):
        for i in range(tiles):
            x = g_ref[s * n + t * i : s * n + t * i + t]
            x = pltpu.roll(x, n, 1) if s else x
            both.append(jnp.where(left, x, jnp.where(lane == sub + (t * i + n), 1.0, 0.0)))

    for top in range(tiles):
        first, live, out = top * t, tiles - top, []
        for s in range(2):
            a = list(both[s * live : (s + 1) * live])
            forward = full = a[0]
            c = [spread(full[:, first + j : first + j + 1]) for j in range(t)]
            pivots = None
            for j in range(t):
                d = spread(c[j][j : j + 1])
                pivots = d if j == 0 else jnp.where(sub == j, d, pivots)
                scale = 1.0 / d
                factor = c[j] * scale
                row = spread(forward[j : j + 1])
                full = jnp.where(sub == j, row * scale, full - factor * row)
                forward = forward - jnp.where(sub > j, factor, 0.0) * row
                for q in range(j + 1, t):
                    value = spread(c[j][q : q + 1])
                    c[q] = jnp.where(sub == j, value * scale, c[q] - factor * value)
            y = forward * lax.rsqrt(pivots)
            o_ref[pl.ds(s * n + first, t)] = jnp.where(left, 0.0, y) if s else jnp.where(left, pltpu.roll(y, n, 1), 0.0)
            solved = [spread(full[j : j + 1]) for j in range(t)]
            for x in a[1:]:
                columns = [spread(x[:, first + j : first + j + 1]) for j in range(t)]
                for j in range(t):
                    x = x - columns[j] * solved[j]
                out.append(x)
        both = out


def inverse(gram):
    return pl.pallas_call(
        invert,
        out_shape=jax.ShapeDtypeStruct((RANK2, RANK2), F32),
        compiler_params=pltpu.CompilerParams(vmem_limit_bytes=16 * MIB),
        cost_estimate=pl.CostEstimate(flops=64**3, bytes_accessed=6 * MIB, transcendentals=128),
    )(gram)


def store_body(half_ref, own_ref, other_ref, m_hbm, sem):
    copies = []
    for i, ref in enumerate((own_ref, other_ref)):
        half = half_ref[0] if i == 0 else 1 - half_ref[0]
        there = pl.ds(pl.multiple_of(half * HALF, HALF), HALF)
        copies.append(pltpu.make_async_copy(ref, m_hbm.at[0, :, there], sem.at[i]))
        copies[-1].start()
    for copy in copies:
        copy.wait()


def store(half, own, other):
    vmem = pl.BlockSpec(memory_space=pltpu.VMEM)
    return pl.pallas_call(
        store_body,
        in_specs=[pl.BlockSpec(memory_space=pltpu.SMEM), vmem, vmem],
        out_specs=pl.BlockSpec(memory_space=pltpu.HBM),
        out_shape=jax.ShapeDtypeStruct((1, 2, ROWS, COLS), BF),
        scratch_shapes=[pltpu.SemaphoreType.DMA((2,))],
        compiler_params=pltpu.CompilerParams(vmem_limit_bytes=16 * MIB),
        cost_estimate=pl.CostEstimate(flops=0, bytes_accessed=4 * MIB, transcendentals=0),
    )(half, own, other)


def factor_body(half_ref, l_ref, po_ref, pt_ref, p_hbm, f_ref, w_ref, sem):
    inv_t = l_ref[...].T
    hi = inv_t.astype(BF)
    w_ref[:RANK2] = hi
    w_ref[RANK2:] = (inv_t - hi.astype(F32)).astype(BF)
    weights = w_ref[...]
    moves = []
    for which, p_ref in enumerate((po_ref, pt_ref)):
        half = half_ref[0] if which == 0 else 1 - half_ref[0]
        for k in range(HALF // BACK):
            p = p_ref[pl.ds(k * BACK, BACK)]
            f_ref[pl.ds(which * HALF + k * BACK, BACK)] = dot(jnp.concatenate([p, p], axis=1), weights).astype(BF)
        there = pl.ds(pl.multiple_of(half * HALF, HALF), HALF)
        moves.append(pltpu.make_async_copy(f_ref.at[pl.ds(which * HALF, HALF)], p_hbm.at[there], sem.at[which]))
        moves[-1].start()
    for copy in moves:
        copy.wait()


def factor(half, inv, p_own, p_other):
    hbm, vmem = pl.BlockSpec(memory_space=pltpu.HBM), pl.BlockSpec(memory_space=pltpu.VMEM)
    return pl.pallas_call(
        factor_body,
        in_specs=[pl.BlockSpec(memory_space=pltpu.SMEM)] + [vmem] * 3,
        out_specs=[hbm, vmem],
        out_shape=[jax.ShapeDtypeStruct((ROWS, RANK2), BF), pltpu.VMEM((ROWS, RANK2), BF)],
        scratch_shapes=[pltpu.VMEM((2 * RANK2, RANK2), BF), pltpu.SemaphoreType.DMA((2,))],
        compiler_params=pltpu.CompilerParams(vmem_limit_bytes=16 * MIB),
        cost_estimate=pl.CostEstimate(flops=4 * ROWS * 128 * 128, bytes_accessed=6 * MIB, transcendentals=0),
    )(half, inv, p_own, p_other)


def split(x):
    hi = x.astype(BF)
    return hi, (x - hi.astype(F32)).astype(BF)


def back_body(half_ref, f_ref, co_ref, ct_ref, l_ref, u_ref, a_ref, b_ref, d_ref, e_hbm, q_ref, e_buf, w_ref, sem):
    u, a, b, d = (t[...].astype(F32) for t in (u_ref, a_ref, b_ref, d_ref))
    (ih, il), (uh, ul) = split(l_ref[...]), split(((u + a) + (b + d)) * (1.0 / (NZ * NX)))
    qt = dot(jnp.concatenate([ih, il], axis=1), jnp.concatenate([uh, uh], axis=0)) + dot(ih, ul)
    q_ref[...] = qt
    qt = qt.astype(BF)
    top = lax.broadcasted_iota(jnp.int32, qt.shape, 0) < RANK2 // 2
    zero = jnp.zeros_like(qt)
    w_ref[...] = jnp.concatenate([jnp.where(top, qt, zero), jnp.where(top, zero, qt)], axis=1)
    weights = w_ref[...]
    copies = []
    for which, c_ref in enumerate((co_ref, ct_ref)):
        half = half_ref[0] if which == 0 else 1 - half_ref[0]
        for k in range(HALF // BACK):
            here = pl.ds(which * HALF + k * BACK, BACK)
            there = pl.ds(pl.multiple_of(half * HALF + k * BACK, BACK), BACK)
            approx = dot(f_ref[here], weights)
            for group in range(2):
                c = c_ref[group, pl.ds(k * BACK, BACK)].astype(F32)
                e_buf[group, here] = (c - approx[:, group * COLS : (group + 1) * COLS]).astype(BF)
            copies.append(pltpu.make_async_copy(e_buf.at[:, here], e_hbm.at[0, :, there], sem.at[which, k]))
            copies[-1].start()
    q_ref[...] = q_ref[...].T
    for copy in copies:
        copy.wait()


def back(half, f, c_own, c_other, inv, us):
    vmem = pl.BlockSpec(memory_space=pltpu.VMEM)
    return pl.pallas_call(
        back_body,
        in_specs=[pl.BlockSpec(memory_space=pltpu.SMEM)] + [vmem] * 8,
        out_specs=[pl.BlockSpec(memory_space=pltpu.HBM), vmem],
        out_shape=[
            jax.ShapeDtypeStruct((1, 2, ROWS, COLS), BF),
            jax.ShapeDtypeStruct((COLS, RANK2), F32),
        ],
        scratch_shapes=[
            pltpu.VMEM((2, ROWS, COLS), BF),
            pltpu.VMEM((RANK2, 2 * COLS), BF),
            pltpu.SemaphoreType.DMA((2, HALF // BACK)),
        ],
        compiler_params=pltpu.CompilerParams(vmem_limit_bytes=16 * MIB),
        cost_estimate=pl.CostEstimate(flops=4 * ROWS * 128 * 128, bytes_accessed=6 * MIB, transcendentals=0),
    )(half, f, c_own, c_other, inv, *us)


def swap_cores(x):
    return lax.ppermute(x, "c", [(0, 1), (1, 0)])


def pair(x, axis, size, flip):
    return lax.ppermute(x, axis, [(i, i ^ flip) for i in range(size)])


def plus(a, b):
    return (a.astype(F32) + b.astype(F32)).astype(BF)


def exchange(x, axes):
    return lax.all_to_all(x, axes, 0, 0)


def local(grads, momentum, error, q_warm):
    c = lax.axis_index("c").astype(jnp.int32)
    mine, theirs = c.reshape(1), (1 - c).reshape(1)

    with jax.named_scope("p_partial"):
        args = (grads, momentum, error, q_warm)
        mo_other, c_other, p_send, *ahead = front(theirs, args, None)
        p_got = swap_cores(p_send)
        mo_own, c_own, p_own = front(mine, args, ahead)
        chip = (p_own + p_got.astype(F32)).astype(BF)
    with jax.named_scope("p_sum"):
        parts = exchange(chip.reshape(NX * NY, BLK, RANK2), ("y", "x"))
        part = sum_copies(parts, 1)[0]
        part = plus(part, pair(part, "z", NZ, 6))
        got = [pair(part, "z", NZ, k) for k in (1, 2, 3)]
        got, momentum_out = lax.optimization_barrier((got, store(mine, mo_own, mo_other)))
        parts = jnp.stack([part] + got)
        p_mine = exchange(sum_copies(parts, NX * NY), ("y", "x")).reshape(HALF, RANK2)
        p_theirs = swap_cores(p_mine)
    with jax.named_scope("u_sum"):
        first = products(p_mine, c_own, None)
        u, gram = products(p_theirs, c_other, first)
        def tree(u, got):
            u, a, b, d = (t.astype(F32) for t in (u, *got))
            return ((u + a) + (b + d)).astype(BF)

        got = pair(u, "z", NZ, 6)
        got, inv = lax.optimization_barrier((got, inverse(gram)))
        u = plus(u, got)
        got = [pair(u, "z", NZ, k) for k in (1, 2, 3)]
        got, p_factor, f = lax.optimization_barrier((got, *factor(mine, inv, p_mine, p_theirs)))
        u = tree(u, got)
        got = [pair(u, "x", NX, k) for k in (1, 3, 2)]
    with jax.named_scope("back"):
        error_out, q_factor = back(mine, f, c_own, c_other, inv, (u, *got))
    return momentum_out, error_out, p_factor, q_factor


def solution(mesh):
    fine = Mesh(mesh.devices.reshape(NZ, NX, NY, NC), ("z", "x", "y", "c"))
    dp, tensor = ("z", "x"), ("y", "c")
    big = P(dp, None, None, tensor)
    return jax.shard_map(
        local,
        mesh=fine,
        in_specs=(big, big, big, P(tensor, None)),
        out_specs=(big, big, P(), P(tensor, None)),
        check_vma=False,
    )
```
